256 devices in a mesh: ctx: 32 (over x_lo, z, core), head: 8 (over x_hi, y).
Axes of the slice: x: 4 (x_hi: 2, x_lo: 2; x = x_hi * 2 + x_lo), y: 4, z: 8, core: 2. Of those that a mesh axis runs over, the one named last changes fastest.
Arguments:
- q_nope: bfloat16 [4096, 16384], P('ctx', 'head'), may hold values from -6 to 6
- q_rope: bfloat16 [4096, 8192], P('ctx', 'head'), may hold values from -32 to 32
- latent: bfloat16 [4096, 576], P(('ctx', 'head')), may hold values from -32 to 32
- block_start: int32 [64], replicated, may hold values from 0 to 4032, as said below
- w_uk: bfloat16 [128, 128, 512], P('head'), may hold values from -0.5 to 0.5
- w_uv: bfloat16 [128, 512, 128], P('head'), may hold values from -1.5 to 1.5
Outputs:
- attn_out: bfloat16 [4096, 16384], P('ctx', 'head')
The draws below stay inside these ranges and needn't reach their ends.
Inputs may be any that keep to these rules, and one draw needn't show every extreme that they name: `block_start`: blocks 2 i and 2 i + 1 start at k * 64 and (63 - k) * 64 for a k that takes each value 0 to 31 once over i.
All inputs are finite; a program needn't handle non-finite values.
Results may differ from the reference program's by a relative error of at most 0.0065.
Values may be sent and summed in bfloat16 or wider, within the bound.
No kernel may reach another device: no remote copies, remote signals or barrier semaphores. Data moves between devices by JAX's collectives and lax.ppermute only.
A program may use at most 128 MiB of HBM per device.

```python
import math
import jax
import jax.numpy as jnp
from jax import lax

HEADS = 128
DN = 128
DR = 64
LAT = 512
DV = 128
BLK = 64
SEQ = 4096
NBLK = 64


def draw_latent(key, part):
    own_key = jax.random.fold_in(key, 1)
    result = jnp.clip(jax.random.normal(own_key, (SEQ, LAT + DR), jnp.float32), -6.0, 6.0)
    return result.astype(jnp.bfloat16)


def draw_q_rope(key, part):
    own_key = jax.random.fold_in(key, 2)
    result = jnp.clip(jax.random.normal(own_key, (SEQ, HEADS * DR), jnp.float32), -6.0, 6.0)
    return result.astype(jnp.bfloat16)


def draw_block_start(key, part):
    order = jax.random.permutation(jax.random.fold_in(key, 3), NBLK // 2).astype(jnp.int32)
    lower_start = order * BLK
    upper_start = (NBLK - 1 - order) * BLK
    return jnp.stack([lower_start, upper_start], axis=1).reshape(NBLK).astype(jnp.int32)


def levels(key, dims, split, smallest, high):
    level, own = 1.0, jax.random.fold_in(key, 6)
    for axis_at, parts in split:
        heights = jnp.exp(jax.random.uniform(jax.random.fold_in(own, axis_at), (parts,), jnp.float32, smallest / len(split), high / len(split)))
        level = level * jnp.repeat(heights, dims[axis_at] // parts).reshape([-1 if axis == axis_at else 1 for axis in range(len(dims))])
    return level


def gaussian(key, shape, width, limit, split=(), kind=jnp.bfloat16):
    drawn = width * jax.random.normal(key, shape, jnp.float32)
    if split:
        drawn = drawn * levels(key, shape, split, -0.22, 0.18)
    return jnp.clip(drawn, -limit, limit).astype(kind)


def setup_inputs(seed: int = 0) -> dict:
    splits = jax.random.split(jax.random.key(seed), 7)
    q_nope = gaussian(splits[0], (SEQ, HEADS * DN), 1.0, 6.0, ((0, 32), (1, 8)))
    q_rope = draw_q_rope(jax.random.fold_in(splits[6], 71), 0)
    latent = draw_latent(jax.random.fold_in(splits[6], 71), 0)
    block_start = draw_block_start(jax.random.fold_in(splits[6], 71), 0)
    w_uk = gaussian(splits[4], (HEADS, DN, LAT), DN ** -0.5, 0.5, ((0, 8),))
    w_uv = gaussian(splits[5], (HEADS, LAT, DV), 0.25, 1.5, ((0, 8),))
    return dict(q_nope=q_nope, q_rope=q_rope, latent=latent, block_start=block_start, w_uk=w_uk, w_uv=w_uv)


def reference(q_nope, q_rope, latent, block_start, w_uk, w_uv):
    rows = jnp.arange(SEQ, dtype=jnp.int32)
    positions_all = jnp.take(block_start, rows // BLK) + rows % BLK
    allowed = positions_all[None, :] <= positions_all[:, None]
    score_scale = 1.0 / math.sqrt(DN + DR)
    nope_heads = q_nope.reshape(SEQ, HEADS, DN)
    rope_heads = q_rope.reshape(SEQ, HEADS, DR)

    def one_head(head_index):
        q_lat = jnp.dot(nope_heads[:, head_index, :], w_uk[head_index], preferred_element_type=jnp.float32).astype(jnp.bfloat16)
        query = jnp.concatenate([q_lat, rope_heads[:, head_index, :]], axis=1)
        scores = jnp.dot(query, latent.T, preferred_element_type=jnp.float32) * score_scale
        top_score = lax.optimization_barrier(jnp.max(jnp.where(allowed, scores, -1e+30), axis=1, keepdims=True))
        weights = jnp.where(allowed, jnp.exp(scores - top_score), 0.0)
        total = lax.optimization_barrier(jnp.sum(weights, axis=1, keepdims=True))
        o_lat = (jnp.dot(weights.astype(jnp.bfloat16), latent[:, :LAT], preferred_element_type=jnp.float32) / total).astype(jnp.bfloat16)
        return jnp.dot(o_lat, w_uv[head_index], preferred_element_type=jnp.float32).astype(jnp.bfloat16)
    outputs = lax.map(one_head, jnp.arange(HEADS, dtype=jnp.int32))
    return jnp.transpose(outputs, (1, 0, 2)).reshape(SEQ, HEADS * DV)
```

```python
import functools
import math

import jax
import jax.numpy as jnp
from jax import lax
from jax.experimental import pallas as pl
from jax.experimental.pallas import tpu as pltpu
from jax.sharding import PartitionSpec as P

BOTH = ("ctx", "head")
PIECE = 16
TILE = 256
OFFSETS = (0, 1, 3, 2)
WINDOW = (0, 1, 7, 3, 4, 2, 5, 6)


def device_index(x, y, z, core):
    return (((x % 2) * 8 + z) * 2 + core) * 8 + (x // 2) * 4 + y


def from_offset(value, first, second):
    pairs = []
    for x in range(4):
        for y in range(4):
            for z in range(8):
                for core in range(2):
                    dx, dy, dz = second if core else first
                    source = device_index((x + dx) % 4, (y + dy) % 4, (z + dz) % 8, core)
                    pairs.append((source, device_index(x, y, z, core)))
    return lax.ppermute(value, BOTH, pairs)


def other_core(value):
    return lax.ppermute(value, "ctx", [(i, i ^ 1) for i in range(32)])


def gather_own_core(latent):
    up = from_offset(latent, (0, 0, 1), (0, 0, 1))
    down = from_offset(latent, (0, 0, 7), (0, 0, 7))
    window = jnp.concatenate([latent, up, down])
    far_up = from_offset(window, (0, 0, 3), (0, 0, 3))
    far_down = from_offset(window[: 2 * PIECE], (0, 0, 5), (0, 0, 5))
    column = jnp.concatenate([window, far_up, far_down])
    plane = jnp.concatenate(
        [column] + [from_offset(column, (0, d, 0), (d, 0, 0)) for d in OFFSETS[1:]]
    )
    return [plane] + [from_offset(plane, (d, 0, 0), (0, d, 0)) for d in OFFSETS[1:]]


def query_kernel(nope_ref, rope_ref, uk_ref, query_ref):
    latent_width = uk_ref.shape[2]
    nope_width = uk_ref.shape[1]
    rope_width = rope_ref.shape[1] // uk_ref.shape[0]
    block = nope_ref.shape[0] // 2
    for head in range(uk_ref.shape[0]):
        lat = jnp.dot(
            nope_ref[:, head * nope_width : (head + 1) * nope_width],
            uk_ref[head],
            preferred_element_type=jnp.float32,
        ).astype(jnp.bfloat16)
        rope = rope_ref[:, head * rope_width : (head + 1) * rope_width]
        for half in range(2):
            rows = slice(half * block, (half + 1) * block)
            to = slice(head * block, (head + 1) * block)
            query_ref[half, to, :latent_width] = lat[rows]
            query_ref[half, to, latent_width:] = rope[rows]


def make_queries(q_nope, q_rope, w_uk):
    rows = q_nope.shape[0]
    heads, nope_width, latent_width = w_uk.shape
    rope_width = q_rope.shape[1] // heads
    at_once = 2
    width = latent_width + rope_width
    return pl.pallas_call(
        query_kernel,
        grid=(heads // at_once,),
        in_specs=[
            pl.BlockSpec((rows, at_once * nope_width), lambda g: (0, g)),
            pl.BlockSpec((rows, at_once * rope_width), lambda g: (0, g)),
            pl.BlockSpec((at_once, nope_width, latent_width), lambda g: (g, 0, 0)),
        ],
        out_specs=pl.BlockSpec((2, at_once * rows // 2, width), lambda g: (0, g, 0)),
        out_shape=jax.ShapeDtypeStruct((2, heads * rows // 2, width), jnp.bfloat16),
        cost_estimate=pl.CostEstimate(
            flops=2 * rows * heads * nope_width * latent_width,
            bytes_accessed=6 * 2**20,
            transcendentals=0,
        ),
        name="make_queries",
    )(q_nope, q_rope, w_uk)


def attention_kernel(starts_ref, query_ref, *refs):
    pieces = refs[:8]
    uv_ref, out_ref, keys, scores, top, total, acc = refs[8:]
    ctx, head_group = lax.axis_index("ctx"), lax.axis_index("head")
    x = (head_group // 4) * 2 + ctx // 16
    y, z, core = head_group % 4, (ctx // 2) % 8, ctx % 2
    count, block, latent_width = uv_ref.shape[0], out_ref.shape[0] // 2, uv_ref.shape[1]
    value_width = uv_ref.shape[2]
    rows = count * block
    factor = math.log2(math.e) / math.sqrt(value_width + query_ref.shape[2] - latent_width)

    for side in range(2):
        owner = core if side == 0 else 1 - core
        for last in range(4):
            ref = pieces[side * 4 + last]
            for middle in range(4):
                px = (x + jnp.where(owner == 0, OFFSETS[last], OFFSETS[middle])) % 4
                py = (y + jnp.where(owner == 0, OFFSETS[middle], OFFSETS[last])) % 4
                for first in range(8):
                    pz = (z + WINDOW[first]) % 8
                    token_block = 2 * (((px % 2) * 8 + pz) * 2 + owner) + px // 2
                    to = pl.multiple_of(starts_ref[token_block] + py * PIECE, PIECE)
                    at = (middle * 8 + first) * PIECE
                    keys[pl.ds(to, PIECE), :] = ref[at : at + PIECE, :]

    ahead = lax.broadcasted_iota(jnp.int32, (block, TILE), 0) - lax.broadcasted_iota(
        jnp.int32, (block, TILE), 1
    )
    chunk = 4 * block

    @pl.loop(0, 2)
    def _(half):
        start = starts_ref[2 * ctx + half]
        tiles = start // TILE + 1
        top[...] = jnp.full(top.shape, -1e30, jnp.float32)

        @pl.loop(0, tiles)
        def _(j):
            at = pl.multiple_of(j * TILE, TILE)
            tile = keys[pl.ds(at, TILE), :]
            allowed = ahead >= at - start
            for c in range(rows // chunk):
                own = slice(c * chunk, (c + 1) * chunk)
                s = lax.dot_general(
                    query_ref[half, own, :],
                    tile,
                    (((1,), (1,)), ((), ())),
                    preferred_element_type=jnp.float32,
                )
                s = jnp.where(allowed[None], s.reshape(chunk // block, block, TILE), -1e30)
                s = s.reshape(chunk, TILE)
                scores[own, pl.ds(at, TILE)] = s
                top[own, :] = jnp.maximum(top[own, :], jnp.maximum(s[:, :128], s[:, 128:]))

        top[...] = jnp.broadcast_to(
            jnp.max(top[...], axis=1, keepdims=True) * factor, top.shape
        )
        total[...] = jnp.zeros(total.shape, jnp.float32)
        acc[...] = jnp.zeros(acc.shape, jnp.float32)

        @pl.loop(0, tiles)
        def _(j):
            at = pl.multiple_of(j * TILE, TILE)
            tile = keys[pl.ds(at, TILE), :latent_width]
            for c in range(rows // chunk):
                own = slice(c * chunk, (c + 1) * chunk)
                shift = top[own, :]
                left = jnp.exp2(scores[own, pl.ds(at, 128)] * factor - shift)
                right = jnp.exp2(scores[own, pl.ds(at + 128, 128)] * factor - shift)
                total[own, :] += left + right
                weights = jnp.concatenate([left, right], axis=1).astype(jnp.bfloat16)
                acc[own, :] += jnp.dot(weights, tile, preferred_element_type=jnp.float32)

        to = pl.ds(pl.multiple_of(half * block, block), block)
        for h in range(count):
            own = slice(h * block, (h + 1) * block)
            whole = jnp.sum(total[own, :], axis=1, keepdims=True)
            lat = (acc[own, :] / whole).astype(jnp.bfloat16)
            out_ref[to, h * value_width : (h + 1) * value_width] = jnp.dot(
                lat, uv_ref[h], preferred_element_type=jnp.float32
            ).astype(jnp.bfloat16)


def attend(block_start, query, pieces, w_uv):
    heads, latent_width, value_width = w_uv.shape
    rows = query.shape[1]
    block = rows // heads
    keys = sum(p.shape[0] for p in pieces)
    width = query.shape[2]
    vmem = pl.BlockSpec(memory_space=pltpu.VMEM)
    return pl.pallas_call(
        attention_kernel,
        in_specs=[pl.BlockSpec(memory_space=pltpu.SMEM)] + [vmem] * (2 + len(pieces)),
        out_specs=vmem,
        out_shape=jax.ShapeDtypeStruct((2 * block, heads * value_width), jnp.bfloat16),
        scratch_shapes=[
            pltpu.VMEM((keys, width), jnp.bfloat16),
            pltpu.VMEM((rows, keys), jnp.float32),
            pltpu.VMEM((rows, 128), jnp.float32),
            pltpu.VMEM((rows, 128), jnp.float32),
            pltpu.VMEM((rows, latent_width), jnp.float32),
        ],
        compiler_params=pltpu.CompilerParams(vmem_limit_bytes=50 * 2**20),
        cost_estimate=pl.CostEstimate(
            flops=2 * rows * (keys + 256) * (width + latent_width),
            bytes_accessed=10 * 2**20,
            transcendentals=rows * keys,
        ),
        name="attention",
    )(block_start, query, *pieces, w_uv)


def shards(q_nope, q_rope, latent, block_start, w_uk, w_uv):
    query = make_queries(q_nope, q_rope, w_uk)
    own = gather_own_core(latent)
    pieces = own + [other_core(p) for p in own]
    return attend(block_start, query, pieces, w_uv)


def solution(mesh):
    placed = (P("ctx", "head"), P("ctx", "head"), P(BOTH, None), P(), P("head"), P("head"))
    return jax.shard_map(
        shards, mesh=mesh, in_specs=placed, out_specs=P("ctx", "head"), check_vma=False
    )
```

```python
import functools
import math

import jax
import jax.numpy as jnp
from jax import lax
from jax.experimental import pallas as pl
from jax.experimental.pallas import tpu as pltpu
from jax.sharding import PartitionSpec as P

BOTH = ("ctx", "head")
PIECE = 16
TILE = 512
OFFSETS = (0, 1, 3, 2)
WINDOW = (0, 1, 7, 3, 4, 2, 5, 6)


def device_index(x, y, z, core):
    return (((x % 2) * 8 + z) * 2 + core) * 8 + (x // 2) * 4 + y


def from_offset(value, first, second):
    pairs = []
    for x in range(4):
        for y in range(4):
            for z in range(8):
                for core in range(2):
                    dx, dy, dz = second if core else first
                    source = device_index((x + dx) % 4, (y + dy) % 4, (z + dz) % 8, core)
                    pairs.append((source, device_index(x, y, z, core)))
    return lax.ppermute(value, BOTH, pairs)


def other_core(value):
    return lax.ppermute(value, "ctx", [(i, i ^ 1) for i in range(32)])


def gather_own_core(latent, query):
    latent = latent[None]
    up = from_offset(latent, (0, 0, 1), (0, 0, 1))
    down = from_offset(latent, (0, 0, 7), (0, 0, 7))
    window = jnp.concatenate([latent, up, down])
    far_up = from_offset(window, (0, 0, 3), (0, 0, 3))
    far_down = from_offset(window[:2], (0, 0, 5), (0, 0, 5))
    column = jnp.concatenate([window, far_up, far_down])
    plane = jnp.concatenate(
        [column] + [from_offset(column, (0, d, 0), (d, 0, 0)) for d in OFFSETS[1:]]
    )
    plane, query = lax.optimization_barrier((plane, query))
    own = [plane] + [from_offset(plane, (d, 0, 0), (0, d, 0)) for d in OFFSETS[1:]]
    return own, query


def query_kernel(nope_ref, rope_ref, uk_ref, query_ref):
    latent_width = uk_ref.shape[2]
    nope_width = uk_ref.shape[1]
    rope_width = rope_ref.shape[1] // uk_ref.shape[0]
    block = nope_ref.shape[0] // 2
    for head in range(uk_ref.shape[0]):
        lat = jnp.dot(
            nope_ref[:, head * nope_width : (head + 1) * nope_width],
            uk_ref[head],
            preferred_element_type=jnp.float32,
        ).astype(jnp.bfloat16)
        rope = rope_ref[:, head * rope_width : (head + 1) * rope_width]
        for half in range(2):
            rows = slice(half * block, (half + 1) * block)
            to = slice(head * block, (head + 1) * block)
            query_ref[half, to, :latent_width] = lat[rows]
            query_ref[half, to, latent_width:] = rope[rows]


def make_queries(q_nope, q_rope, w_uk):
    rows = q_nope.shape[0]
    heads, nope_width, latent_width = w_uk.shape
    rope_width = q_rope.shape[1] // heads
    at_once = 2
    width = latent_width + rope_width
    return pl.pallas_call(
        query_kernel,
        grid=(heads // at_once,),
        in_specs=[
            pl.BlockSpec((rows, at_once * nope_width), lambda g: (0, g)),
            pl.BlockSpec((rows, at_once * rope_width), lambda g: (0, g)),
            pl.BlockSpec((at_once, nope_width, latent_width), lambda g: (g, 0, 0)),
        ],
        out_specs=pl.BlockSpec((2, at_once * rows // 2, width), lambda g: (0, g, 0)),
        out_shape=jax.ShapeDtypeStruct((2, heads * rows // 2, width), jnp.bfloat16),
        cost_estimate=pl.CostEstimate(
            flops=2 * rows * heads * nope_width * latent_width,
            bytes_accessed=6 * 2**20,
            transcendentals=0,
        ),
        name="make_queries",
    )(q_nope, q_rope, w_uk)


def attention_kernel(starts_ref, query_ref, *refs):
    pieces = refs[:8]
    uv_ref, out_ref, keys, scores, top, total, acc = refs[8:]
    ctx, head_group = lax.axis_index("ctx"), lax.axis_index("head")
    x = (head_group // 4) * 2 + ctx // 16
    y, z, core = head_group % 4, (ctx // 2) % 8, ctx % 2
    count, block, latent_width = uv_ref.shape[0], out_ref.shape[0] // 2, uv_ref.shape[1]
    value_width = uv_ref.shape[2]
    rows = count * block
    factor = math.log2(math.e) / math.sqrt(value_width + query_ref.shape[2] - latent_width)

    for side in range(2):
        owner = core if side == 0 else 1 - core
        for last in range(4):
            ref = pieces[side * 4 + last]
            for middle in range(4):
                px = (x + jnp.where(owner == 0, OFFSETS[last], OFFSETS[middle])) % 4
                py = (y + jnp.where(owner == 0, OFFSETS[middle], OFFSETS[last])) % 4
                for first in range(8):
                    pz = (z + WINDOW[first]) % 8
                    token_block = 2 * (((px % 2) * 8 + pz) * 2 + owner) + px // 2
                    to = pl.multiple_of(starts_ref[token_block] + py * PIECE, PIECE)
                    keys[pl.ds(to, PIECE), :] = ref[middle * 8 + first]

    ahead = lax.broadcasted_iota(jnp.int32, (block, TILE), 0) - lax.broadcasted_iota(
        jnp.int32, (block, TILE), 1
    )
    chunk = 16 * block

    @pl.loop(0, 2)
    def _(half):
        start = starts_ref[2 * ctx + half]
        tiles = start // TILE + 1
        top[...] = jnp.full(top.shape, -1e30, jnp.float32)

        @pl.loop(0, tiles)
        def _(j):
            at = pl.multiple_of(j * TILE, TILE)
            tile = keys[pl.ds(at, TILE), :]
            allowed = ahead >= at - start
            for c in range(rows // chunk):
                own = slice(c * chunk, (c + 1) * chunk)
                s = lax.dot_general(
                    query_ref[half, own, :],
                    tile,
                    (((1,), (1,)), ((), ())),
                    preferred_element_type=jnp.float32,
                )
                s = jnp.where(allowed[None], s.reshape(chunk // block, block, TILE), -1e30)
                s = s.reshape(chunk, TILE)
                scores[own, pl.ds(at, TILE)] = s
                top[own, :] = functools.reduce(jnp.maximum, [s[:, i:i+128] for i in range(0, TILE, 128)], top[own, :])

        top[...] = jnp.broadcast_to(
            jnp.max(top[...], axis=1, keepdims=True) * factor, top.shape
        )
        total[...] = jnp.zeros(total.shape, jnp.float32)
        acc[...] = jnp.zeros(acc.shape, jnp.float32)

        @pl.loop(0, tiles)
        def _(j):
            at = pl.multiple_of(j * TILE, TILE)
            tile = keys[pl.ds(at, TILE), :latent_width]
            for c in range(rows // chunk):
                own = slice(c * chunk, (c + 1) * chunk)
                shift = top[own, :]
                parts = [jnp.exp2(scores[own, pl.ds(at + i, 128)] * factor - shift) for i in range(0, TILE, 128)]
                total[own, :] += sum(parts[1:], parts[0])
                weights = jnp.concatenate(parts, axis=1).astype(jnp.bfloat16)
                acc[own, :] += jnp.dot(weights, tile, preferred_element_type=jnp.float32)

        to = pl.ds(pl.multiple_of(half * block, block), block)
        for h in range(count):
            own = slice(h * block, (h + 1) * block)
            whole = jnp.sum(total[own, :], axis=1, keepdims=True)
            lat = (acc[own, :] / whole).astype(jnp.bfloat16)
            out_ref[to, h * value_width : (h + 1) * value_width] = jnp.dot(
                lat, uv_ref[h], preferred_element_type=jnp.float32
            ).astype(jnp.bfloat16)


def attend(block_start, query, pieces, w_uv):
    heads, latent_width, value_width = w_uv.shape
    rows = query.shape[1]
    block = rows // heads
    keys = sum(p.shape[0] * p.shape[1] for p in pieces)
    width = query.shape[2]
    vmem = pl.BlockSpec(memory_space=pltpu.VMEM)
    return pl.pallas_call(
        attention_kernel,
        in_specs=[pl.BlockSpec(memory_space=pltpu.SMEM)] + [vmem] * (2 + len(pieces)),
        out_specs=vmem,
        out_shape=jax.ShapeDtypeStruct((2 * block, heads * value_width), jnp.bfloat16),
        scratch_shapes=[
            pltpu.VMEM((keys, width), jnp.bfloat16),
            pltpu.VMEM((rows, keys), jnp.float32),
            pltpu.VMEM((rows, 128), jnp.float32),
            pltpu.VMEM((rows, 128), jnp.float32),
            pltpu.VMEM((rows, latent_width), jnp.float32),
        ],
        compiler_params=pltpu.CompilerParams(vmem_limit_bytes=30 * 2**20),
        cost_estimate=pl.CostEstimate(
            flops=2 * rows * (keys + 256) * (width + latent_width),
            bytes_accessed=10 * 2**20,
            transcendentals=rows * keys,
        ),
        name="attention",
    )(block_start, query, *pieces, w_uv)


def shards(q_nope, q_rope, latent, block_start, w_uk, w_uv):
    query = make_queries(q_nope, q_rope, w_uk)
    own, query = gather_own_core(latent, query)
    pieces = own + [other_core(p) for p in own]
    return attend(block_start, query, pieces, w_uv)


def solution(mesh):
    placed = (P("ctx", "head"), P("ctx", "head"), P(BOTH, None), P(), P("head"), P("head"))
    return jax.shard_map(
        shards, mesh=mesh, in_specs=placed, out_specs=P("ctx", "head"), check_vma=False
    )
```

```python
import functools
import math

import jax
import jax.numpy as jnp
from jax import lax
from jax.experimental import pallas as pl
from jax.experimental.pallas import tpu as pltpu
from jax.sharding import PartitionSpec as P

BOTH = ("ctx", "head")
PIECE = 16
TILE = 256
CHUNK = 1024
NOPE = 128
OFFSETS = (0, 1, 3, 2)
WINDOW = (0, 1, 7, 3, 4, 2, 5, 6)


def device_index(x, y, z, core):
    return (((x % 2) * 8 + z) * 2 + core) * 8 + (x // 2) * 4 + y


def from_offset(value, first, second):
    pairs = []
    for x in range(4):
        for y in range(4):
            for z in range(8):
                for core in range(2):
                    dx, dy, dz = second if core else first
                    source = device_index((x + dx) % 4, (y + dy) % 4, (z + dz) % 8, core)
                    pairs.append((source, device_index(x, y, z, core)))
    return lax.ppermute(value, BOTH, pairs)


def other_core(value):
    return lax.ppermute(value, "ctx", [(i, i ^ 1) for i in range(32)])


def gather_own_core(latent, query):
    latent = latent[None]
    up = from_offset(latent, (0, 0, 1), (0, 0, 1))
    down = from_offset(latent, (0, 0, 7), (0, 0, 7))
    window = jnp.concatenate([latent, up, down])
    far_up = from_offset(window, (0, 0, 3), (0, 0, 3))
    far_down = from_offset(window, (0, 0, 5), (0, 0, 5))[:2]
    column = jnp.concatenate([window, far_up, far_down])
    column, query = lax.optimization_barrier((column, query))
    plane = jnp.concatenate(
        [column] + [from_offset(column, (0, d, 0), (d, 0, 0)) for d in OFFSETS[1:]]
    )
    own = [plane] + [from_offset(plane, (d, 0, 0), (0, d, 0)) for d in OFFSETS[1:]]
    return own, query


def query_kernel(nope_ref, rope_ref, uk_ref, query_ref):
    latent_width = uk_ref.shape[2]
    nope_width = uk_ref.shape[1]
    rope_width = rope_ref.shape[1] // uk_ref.shape[0]
    block = nope_ref.shape[0] // 2
    for head in range(uk_ref.shape[0]):
        lat = jnp.dot(
            nope_ref[:, head * nope_width : (head + 1) * nope_width],
            uk_ref[head],
            preferred_element_type=jnp.float32,
        ).astype(jnp.bfloat16)
        rope = rope_ref[:, head * rope_width : (head + 1) * rope_width]
        for half in range(2):
            rows = slice(half * block, (half + 1) * block)
            to = slice(head * block, (head + 1) * block)
            query_ref[half, to, :latent_width] = lat[rows]
            query_ref[half, to, latent_width:] = rope[rows]


def make_queries(q_nope, q_rope, w_uk):
    rows = q_nope.shape[0]
    heads, nope_width, latent_width = w_uk.shape
    rope_width = q_rope.shape[1] // heads
    at_once = 4
    width = latent_width + rope_width
    return pl.pallas_call(
        query_kernel,
        grid=(heads // at_once,),
        in_specs=[
            pl.BlockSpec((rows, at_once * nope_width), lambda g: (0, g)),
            pl.BlockSpec((rows, at_once * rope_width), lambda g: (0, g)),
            pl.BlockSpec((at_once, nope_width, latent_width), lambda g: (g, 0, 0)),
        ],
        out_specs=pl.BlockSpec((2, at_once * rows // 2, width), lambda g: (0, g, 0)),
        out_shape=jax.ShapeDtypeStruct((2, heads * rows // 2, width), jnp.bfloat16),
        cost_estimate=pl.CostEstimate(
            flops=2 * rows * heads * nope_width * latent_width,
            bytes_accessed=6 * 2**20,
            transcendentals=0,
        ),
        name="make_queries",
    )(q_nope, q_rope, w_uk)


def absorb_kernel(last, finish, starts_ref, query_ref, own_ref, other_ref, *refs):
    state_in = refs[: 3 if last else 0]
    refs = refs[len(state_in) :]
    if finish:
        uv_ref, out_ref, keys, marks, acc, top, total = refs
    else:
        acc, top, total, keys, marks = refs
    ctx, head_group = lax.axis_index("ctx"), lax.axis_index("head")
    x = (head_group // 4) * 2 + ctx // 16
    y, z, core = head_group % 4, (ctx // 2) % 8, ctx % 2
    rows = query_ref.shape[1]
    block, width = 4 * PIECE, query_ref.shape[2]
    latent_width = acc.shape[1]
    factor = math.log2(math.e) / math.sqrt(NOPE + width - latent_width)
    low, high = starts_ref[2 * ctx], starts_ref[2 * ctx + 1]

    def column(owner, middle, first):
        px = (x + jnp.where(owner == 0, OFFSETS[last], OFFSETS[middle])) % 4
        py = (y + jnp.where(owner == 0, OFFSETS[middle], OFFSETS[last])) % 4
        pz = (z + WINDOW[first]) % 8
        return starts_ref[2 * (((px % 2) * 8 + pz) * 2 + owner) + px // 2], py

    pieces = []
    for ref, owner in ((own_ref, core), (other_ref, 1 - core)):
        for middle in range(4):
            for first in range(8):
                start, py = column(owner, middle, first)
                pieces.append((ref, middle * 8 + first, start, py))
    below = sum([jnp.where(p[2] <= low, 1, 0) for p in pieces[1:]], jnp.where(pieces[0][2] <= low, 1, 0))
    keys[...] = jnp.zeros(keys.shape, keys.dtype)
    marks[...] = jnp.full(marks.shape, 64.0, marks.dtype)
    lane = lax.broadcasted_iota(jnp.int32, (PIECE, 128), 1)
    row = lax.broadcasted_iota(jnp.int32, (PIECE, 128), 0)
    next_low, next_high = jnp.int32(0), below
    for ref, at, start, py in pieces:
        is_low = start <= low
        is_high = (start > low) & (start <= high)
        to = pl.multiple_of(
            jnp.where(is_low, next_low, jnp.where(is_high, next_high, len(pieces))) * PIECE, PIECE
        )
        keys[pl.ds(to, PIECE), :] = ref[at]
        mark = jnp.where(lane == 0, start // 64, jnp.where(lane == 1, row + py * PIECE, 0))
        marks[pl.ds(to, PIECE), :] = mark.astype(jnp.float32).astype(jnp.bfloat16)
        next_low = next_low + jnp.where(is_low, 1, 0)
        next_high = next_high + jnp.where(is_high, 1, 0)

    if last:
        for to_ref, from_ref in zip((acc, top, total), state_in):
            to_ref[...] = from_ref[...]
    else:
        top[...] = jnp.full(top.shape, -1e30, jnp.float32)
        total[...] = jnp.zeros(total.shape, jnp.float32)
        acc[...] = jnp.zeros(acc.shape, jnp.float32)

    read_lane = lax.broadcasted_iota(jnp.int32, (PIECE, 128), 1)
    read = jnp.where(read_lane == 0, 64.0, jnp.where(read_lane == 1, 1.0, 0.0)).astype(jnp.bfloat16)
    query_row = lax.broadcasted_iota(jnp.int32, (block, TILE), 0).astype(jnp.float32)
    per_tile = TILE // PIECE
    tiles_low = (below + per_tile - 1) // per_tile
    tiles_high = (next_high + per_tile - 1) // per_tile

    @pl.loop(0, tiles_low + tiles_high)
    def _(step):
        is_high = step >= tiles_low
        half = jnp.where(is_high, 1, 0)
        at = pl.multiple_of((step - half * tiles_low) * TILE, TILE)
        start = jnp.where(is_high, high, low)
        tile = keys[pl.ds(at, TILE), :]
        position = lax.dot_general(
            read, marks[pl.ds(at, TILE), :], (((1,), (1,)), ((), ())),
            preferred_element_type=jnp.float32,
        )
        position = jnp.broadcast_to(position[:1, :], (block, TILE))
        allowed = position - start.astype(jnp.float32) <= query_row
        for c in range(rows // CHUNK):
            s = lax.dot_general(
                query_ref[half, c * CHUNK : (c + 1) * CHUNK, :],
                tile,
                (((1,), (1,)), ((), ())),
                preferred_element_type=jnp.float32,
            )
            s = jnp.where(allowed[None], s.reshape(CHUNK // block, block, TILE), -1e30)
            s = s.reshape(CHUNK, TILE)
            own = pl.ds(pl.multiple_of(half * rows + c * CHUNK, CHUNK), CHUNK)
            left, right = s[:, :128], s[:, 128:]
            old = top[own, :]
            new = jnp.maximum(old, jnp.max(jnp.maximum(left, right), axis=1, keepdims=True))
            scale = jnp.exp2((old - new) * factor)
            left = jnp.exp2((left - new) * factor)
            right = jnp.exp2((right - new) * factor)
            top[own, :] = new
            total[own, :] = total[own, :] * scale + (left + right)
            weights = jnp.concatenate([left, right], axis=1).astype(jnp.bfloat16)
            scales = jnp.concatenate([scale] * (latent_width // 128), axis=1)
            acc[own, :] = acc[own, :] * scales + jnp.dot(
                weights, tile[:, :latent_width], preferred_element_type=jnp.float32
            )

    if finish:
        value_width = uv_ref.shape[2]
        for h in range(uv_ref.shape[0]):
            lat = []
            for half in range(2):
                own = slice(half * rows + h * block, half * rows + (h + 1) * block)
                whole = jnp.sum(total[own, :], axis=1, keepdims=True)
                lat.append((acc[own, :] / whole).astype(jnp.bfloat16))
            out_ref[:, h * value_width : (h + 1) * value_width] = jnp.dot(
                jnp.concatenate(lat), uv_ref[h], preferred_element_type=jnp.float32
            ).astype(jnp.bfloat16)


def absorb(last, block_start, query, own, other, state, w_uv):
    heads, latent_width, value_width = w_uv.shape
    rows, width = query.shape[1:]
    finish = last == len(OFFSETS) - 1
    count = 2 * own.shape[0] * own.shape[1]
    vmem = pl.BlockSpec(memory_space=pltpu.VMEM)
    state_shapes = [(2 * rows, latent_width), (2 * rows, 128), (2 * rows, 128)]
    scratch = [
        pltpu.VMEM((count + PIECE, width), jnp.bfloat16),
        pltpu.VMEM((count + PIECE, 128), jnp.bfloat16),
    ]
    operands = [block_start, query, own, other, *state]
    if finish:
        operands.append(w_uv)
        scratch += [pltpu.VMEM(shape, jnp.float32) for shape in state_shapes]
        out_shape = jax.ShapeDtypeStruct((2 * rows // heads, heads * value_width), jnp.bfloat16)
    else:
        out_shape = [jax.ShapeDtypeStruct(shape, jnp.float32) for shape in state_shapes]
    return pl.pallas_call(
        functools.partial(absorb_kernel, last, finish),
        in_specs=[pl.BlockSpec(memory_space=pltpu.SMEM)] + [vmem] * (len(operands) - 1),
        out_specs=vmem if finish else [vmem] * 3,
        out_shape=out_shape,
        scratch_shapes=scratch,
        compiler_params=pltpu.CompilerParams(vmem_limit_bytes=24 * 2**20),
        cost_estimate=pl.CostEstimate(
            flops=rows * count * width,
            bytes_accessed=2**20,
            transcendentals=0,
        ),
        name=f"absorb_{last}",
    )(*operands)


def shards(q_nope, q_rope, latent, block_start, w_uk, w_uv):
    query = make_queries(q_nope, q_rope, w_uk)
    own, query = gather_own_core(latent, query)
    state = ()
    for last, piece in enumerate(own):
        if last:
            piece, state = lax.optimization_barrier((piece, state))
        state = absorb(last, block_start, query, piece, other_core(piece), state, w_uv)
    return state


def solution(mesh):
    placed = (P("ctx", "head"), P("ctx", "head"), P(BOTH, None), P(), P("head"), P("head"))
    return jax.shard_map(
        shards, mesh=mesh, in_specs=placed, out_specs=P("ctx", "head"), check_vma=False
    )
```

```python
import functools
import math

import jax
import jax.numpy as jnp
from jax import lax
from jax.experimental import pallas as pl
from jax.experimental.pallas import tpu as pltpu
from jax.sharding import PartitionSpec as P

BOTH = ("ctx", "head")
PIECE = 16
TILE = 256
CHUNK = 1024
QCHUNK = 1024
OFFSETS = (0, 1, 3, 2)
WINDOW = (0, 1, 7, 3, 4, 2, 5, 6)


def device_index(x, y, z, core):
    return (((x % 2) * 8 + z) * 2 + core) * 8 + (x // 2) * 4 + y


def from_offset(value, first, second):
    pairs = []
    for x in range(4):
        for y in range(4):
            for z in range(8):
                for core in range(2):
                    dx, dy, dz = second if core else first
                    source = device_index((x + dx) % 4, (y + dy) % 4, (z + dz) % 8, core)
                    pairs.append((source, device_index(x, y, z, core)))
    return lax.ppermute(value, BOTH, pairs)


def other_core(value):
    return lax.ppermute(value, "ctx", [(i, i ^ 1) for i in range(32)])


def gather_own_core(latent, query):
    latent = latent[None]
    up = from_offset(latent, (0, 0, 1), (0, 0, 1))
    down = from_offset(latent, (0, 0, 7), (0, 0, 7))
    window = jnp.concatenate([latent, up, down])
    far_up = from_offset(window, (0, 0, 3), (0, 0, 3))
    far_down = from_offset(window, (0, 0, 5), (0, 0, 5))[:2]
    column = jnp.concatenate([window, far_up, far_down])
    plane = jnp.concatenate(
        [column] + [from_offset(column, (0, d, 0), (d, 0, 0)) for d in OFFSETS[1:]]
    )
    lines = [from_offset(plane, (d, 0, 0), (0, d, 0)) for d in OFFSETS[1:]]
    *lines, query = lax.optimization_barrier((*lines, query))
    return [plane, *lines], query


def query_kernel(nope_ref, rope_ref, uk_ref, query_ref):
    latent_width = uk_ref.shape[2]
    nope_width = uk_ref.shape[1]
    rope_width = rope_ref.shape[1] // uk_ref.shape[0]
    block = nope_ref.shape[0] // 2
    for head in range(uk_ref.shape[0]):
        lat = jnp.dot(
            nope_ref[:, head * nope_width : (head + 1) * nope_width],
            uk_ref[head],
            preferred_element_type=jnp.float32,
        ).astype(jnp.bfloat16)
        rope = rope_ref[:, head * rope_width : (head + 1) * rope_width]
        for half in range(2):
            rows = slice(half * block, (half + 1) * block)
            to = slice(head * block, (head + 1) * block)
            query_ref[half, to, :latent_width] = lat[rows]
            query_ref[half, to, latent_width:] = rope[rows]


def make_queries(q_nope, q_rope, w_uk):
    rows = q_nope.shape[0]
    heads, nope_width, latent_width = w_uk.shape
    rope_width = q_rope.shape[1] // heads
    width = latent_width + rope_width
    vmem = pl.BlockSpec(memory_space=pltpu.VMEM)
    return pl.pallas_call(
        query_kernel,
        in_specs=[vmem] * 3,
        out_specs=vmem,
        out_shape=jax.ShapeDtypeStruct((2, heads * rows // 2, width), jnp.bfloat16),
        compiler_params=pltpu.CompilerParams(vmem_limit_bytes=12 * 2**20),
        cost_estimate=pl.CostEstimate(
            flops=2 * rows * heads * nope_width * latent_width,
            bytes_accessed=6 * 2**20,
            transcendentals=0,
        ),
        name="make_queries",
    )(q_nope, q_rope, w_uk)


def attention_kernel(starts_ref, query_ref, *refs):
    pieces = refs[:8]
    uv_ref, out_ref, keys, even, odd, top, total, acc = refs[8:]
    ctx, head_group = lax.axis_index("ctx"), lax.axis_index("head")
    x = (head_group // 4) * 2 + ctx // 16
    y, z, core = head_group % 4, (ctx // 2) % 8, ctx % 2
    count, block, latent_width = uv_ref.shape[0], out_ref.shape[0] // 2, uv_ref.shape[1]
    value_width = uv_ref.shape[2]
    rows = count * block
    factor = math.log2(math.e) / math.sqrt(value_width + query_ref.shape[2] - latent_width)

    for side in range(2):
        owner = core if side == 0 else 1 - core
        for last in range(4):
            ref = pieces[side * 4 + last]
            for middle in range(4):
                px = (x + jnp.where(owner == 0, OFFSETS[last], OFFSETS[middle])) % 4
                py = (y + jnp.where(owner == 0, OFFSETS[middle], OFFSETS[last])) % 4
                for first in range(8):
                    pz = (z + WINDOW[first]) % 8
                    token_block = 2 * (((px % 2) * 8 + pz) * 2 + owner) + px // 2
                    to = pl.multiple_of(starts_ref[token_block] + py * PIECE, PIECE)
                    keys[pl.ds(to, PIECE), :] = ref[middle * 8 + first]

    ahead = lax.broadcasted_iota(jnp.int32, (block, TILE), 0) - lax.broadcasted_iota(
        jnp.int32, (block, TILE), 1
    )
    chunk = CHUNK
    start0, start1 = starts_ref[2 * ctx], starts_ref[2 * ctx + 1]
    steps0, steps1 = start0 // (2 * TILE) + 1, start1 // (2 * TILE) + 1

    def place(step):
        half = jnp.where(step >= steps0, 1, 0)
        start = jnp.where(half == 1, start1, start0)
        return half, start, (step - half * steps0) * (2 * TILE)

    def score(buffer, half, start, at):
        at = pl.multiple_of(jnp.minimum(at, keys.shape[0] - TILE), TILE)
        tile = keys[pl.ds(at, TILE), :]
        allowed = ahead >= at - start
        for c in range(rows // QCHUNK):
            own = slice(c * QCHUNK, (c + 1) * QCHUNK)
            s = lax.dot_general(
                query_ref[half, own, :],
                tile,
                (((1,), (1,)), ((), ())),
                preferred_element_type=jnp.float32,
            )
            s = jnp.where(allowed[None], s.reshape(QCHUNK // block, block, TILE), -1e30)
            buffer[own, :] = s.reshape(QCHUNK, TILE)

    def absorb(buffer, at):
        tile = keys[pl.ds(pl.multiple_of(at, TILE), TILE), :latent_width]
        for c in range(rows // chunk):
            own = slice(c * chunk, (c + 1) * chunk)
            left, right = buffer[own, :128], buffer[own, 128:]
            old = top[own, :]
            new = jnp.maximum(old, jnp.max(jnp.maximum(left, right), axis=1, keepdims=True))
            scale = jnp.exp2((old - new) * factor)
            left = jnp.exp2((left - new) * factor)
            right = jnp.exp2((right - new) * factor)
            top[own, :] = new
            total[own, :] = total[own, :] * scale + (left + right)
            weights = jnp.concatenate([left, right], axis=1).astype(jnp.bfloat16)
            scales = jnp.concatenate([scale] * (latent_width // 128), axis=1)
            acc[own, :] = acc[own, :] * scales + jnp.dot(
                weights, tile, preferred_element_type=jnp.float32
            )

    def clear():
        top[...] = jnp.full(top.shape, -1e30, jnp.float32)
        total[...] = jnp.zeros(total.shape, jnp.float32)
        acc[...] = jnp.zeros(acc.shape, jnp.float32)

    clear()
    score(even, 0, start0, 0)

    @pl.loop(0, steps0 + steps1)
    def _(step):
        half, start, at = place(step)
        score(odd, half, start, at + TILE)
        absorb(even, at)
        half_next, start_next, at_next = place(step + 1)
        score(even, half_next, start_next, at_next)
        absorb(odd, at + TILE)

        @pl.when((step == steps0 - 1) | (step == steps0 + steps1 - 1))
        def _():
            to = pl.ds(pl.multiple_of(half * block, block), block)
            for h in range(count):
                own = slice(h * block, (h + 1) * block)
                whole = jnp.sum(total[own, :], axis=1, keepdims=True)
                lat = (acc[own, :] / whole).astype(jnp.bfloat16)
                out_ref[to, h * value_width : (h + 1) * value_width] = jnp.dot(
                    lat, uv_ref[h], preferred_element_type=jnp.float32
                ).astype(jnp.bfloat16)
            clear()


def attend(block_start, query, pieces, w_uv):
    heads, latent_width, value_width = w_uv.shape
    rows = query.shape[1]
    block = rows // heads
    keys = sum(p.shape[0] * p.shape[1] for p in pieces)
    width = query.shape[2]
    vmem = pl.BlockSpec(memory_space=pltpu.VMEM)
    return pl.pallas_call(
        attention_kernel,
        in_specs=[pl.BlockSpec(memory_space=pltpu.SMEM)] + [vmem] * (2 + len(pieces)),
        out_specs=vmem,
        out_shape=jax.ShapeDtypeStruct((2 * block, heads * value_width), jnp.bfloat16),
        scratch_shapes=[
            pltpu.VMEM((keys, width), jnp.bfloat16),
            pltpu.VMEM((rows, TILE), jnp.float32),
            pltpu.VMEM((rows, TILE), jnp.float32),
            pltpu.VMEM((rows, 128), jnp.float32),
            pltpu.VMEM((rows, 128), jnp.float32),
            pltpu.VMEM((rows, latent_width), jnp.float32),
        ],
        compiler_params=pltpu.CompilerParams(vmem_limit_bytes=20 * 2**20),
        cost_estimate=pl.CostEstimate(
            flops=2 * rows * (keys + 256) * (width + latent_width),
            bytes_accessed=10 * 2**20,
            transcendentals=rows * keys,
        ),
        name="attention",
    )(block_start, query, *pieces, w_uv)


def shards(q_nope, q_rope, latent, block_start, w_uk, w_uv):
    query = make_queries(q_nope, q_rope, w_uk)
    own, query = gather_own_core(latent, query)
    pieces = own + [other_core(p) for p in own]
    return attend(block_start, query, pieces, w_uv)


def solution(mesh):
    placed = (P("ctx", "head"), P("ctx", "head"), P(BOTH, None), P(), P("head"), P("head"))
    return jax.shard_map(
        shards, mesh=mesh, in_specs=placed, out_specs=P("ctx", "head"), check_vma=False
    )
```

```python
import functools
import math

import jax
import jax.numpy as jnp
from jax import lax
from jax.experimental import pallas as pl
from jax.experimental.pallas import tpu as pltpu
from jax.sharding import PartitionSpec as P

BOTH = ("ctx", "head")
PIECE = 16
TILE = 256
NOPE = 128
GROUPS = ((0,), (1, 2), (3,))
OFFSETS = (0, 1, 3, 2)
WINDOW = (0, 1, 7, 3, 4, 2, 5, 6)


def device_index(x, y, z, core):
    return (((x % 2) * 8 + z) * 2 + core) * 8 + (x // 2) * 4 + y


def from_offset(value, first, second):
    pairs = []
    for x in range(4):
        for y in range(4):
            for z in range(8):
                for core in range(2):
                    dx, dy, dz = second if core else first
                    source = device_index((x + dx) % 4, (y + dy) % 4, (z + dz) % 8, core)
                    pairs.append((source, device_index(x, y, z, core)))
    return lax.ppermute(value, BOTH, pairs)


def other_core(value):
    return lax.ppermute(value, "ctx", [(i, i ^ 1) for i in range(32)])


def gather_own_core(latent, query):
    latent = latent[None]
    up = from_offset(latent, (0, 0, 1), (0, 0, 1))
    down = from_offset(latent, (0, 0, 7), (0, 0, 7))
    window = jnp.concatenate([latent, up, down])
    far_up = from_offset(window, (0, 0, 3), (0, 0, 3))
    far_down = from_offset(window, (0, 0, 5), (0, 0, 5))[:2]
    column = jnp.concatenate([window, far_up, far_down])
    column, query = lax.optimization_barrier((column, query))
    plane = jnp.concatenate(
        [column] + [from_offset(column, (0, d, 0), (d, 0, 0)) for d in OFFSETS[1:]]
    )
    lines = [from_offset(plane, (d, 0, 0), (0, d, 0)) for d in OFFSETS[1:]]
    return [plane, *lines], query


def query_kernel(nope_ref, rope_ref, uk_ref, query_ref):
    latent_width = uk_ref.shape[2]
    nope_width = uk_ref.shape[1]
    rope_width = rope_ref.shape[1] // uk_ref.shape[0]
    block = nope_ref.shape[0] // 2
    for head in range(uk_ref.shape[0]):
        lat = jnp.dot(
            nope_ref[:, head * nope_width : (head + 1) * nope_width],
            uk_ref[head],
            preferred_element_type=jnp.float32,
        ).astype(jnp.bfloat16)
        rope = rope_ref[:, head * rope_width : (head + 1) * rope_width]
        for half in range(2):
            rows = slice(half * block, (half + 1) * block)
            to = slice(head * block, (head + 1) * block)
            query_ref[half, to, :latent_width] = lat[rows]
            query_ref[half, to, latent_width:] = rope[rows]


def make_queries(q_nope, q_rope, w_uk):
    rows = q_nope.shape[0]
    heads, nope_width, latent_width = w_uk.shape
    rope_width = q_rope.shape[1] // heads
    width = latent_width + rope_width
    vmem = pl.BlockSpec(memory_space=pltpu.VMEM)
    return pl.pallas_call(
        query_kernel,
        in_specs=[vmem] * 3,
        out_specs=vmem,
        out_shape=jax.ShapeDtypeStruct((2, heads * rows // 2, width), jnp.bfloat16),
        compiler_params=pltpu.CompilerParams(vmem_limit_bytes=12 * 2**20),
        cost_estimate=pl.CostEstimate(
            flops=2 * rows * heads * nope_width * latent_width,
            bytes_accessed=6 * 2**20,
            transcendentals=0,
        ),
        name="make_queries",
    )(q_nope, q_rope, w_uk)


def absorb_kernel(lasts, finish, starts_ref, query_ref, *refs):
    piece_refs, refs = refs[: 2 * len(lasts)], refs[2 * len(lasts) :]
    state_in = refs[: 0 if lasts[0] == 0 else 3]
    refs = refs[len(state_in) :]
    if finish:
        uv_ref, out_ref, keys, marks, even, odd, acc, top, total = refs
    else:
        acc, top, total, keys, marks, even, odd = refs
    ctx, head_group = lax.axis_index("ctx"), lax.axis_index("head")
    x = (head_group // 4) * 2 + ctx // 16
    y, z, core = head_group % 4, (ctx // 2) % 8, ctx % 2
    rows = query_ref.shape[1]
    block, width = 4 * PIECE, query_ref.shape[2]
    latent_width = acc.shape[1]
    factor = math.log2(math.e) / math.sqrt(NOPE + width - latent_width)
    low, high = starts_ref[2 * ctx], starts_ref[2 * ctx + 1]

    if state_in:
        for to_ref, from_ref in zip((acc, top, total), state_in):
            to_ref[...] = from_ref[...]
    else:
        top[...] = jnp.full(top.shape, -1e30, jnp.float32)
        total[...] = jnp.zeros(total.shape, jnp.float32)
        acc[...] = jnp.zeros(acc.shape, jnp.float32)

    pieces = []
    for index, ref in enumerate(piece_refs):
        last, owner = lasts[index // 2], core if index % 2 == 0 else 1 - core
        for middle in range(4):
            px = (x + jnp.where(owner == 0, OFFSETS[last], OFFSETS[middle])) % 4
            py = (y + jnp.where(owner == 0, OFFSETS[middle], OFFSETS[last])) % 4
            for first in range(8):
                pz = (z + WINDOW[first]) % 8
                start = starts_ref[2 * (((px % 2) * 8 + pz) * 2 + owner) + px // 2]
                pieces.append((ref, middle * 8 + first, start, py * PIECE))
    below = jnp.int32(0)
    within = jnp.int32(0)
    for _, _, start, _ in pieces:
        below = below + jnp.where(start <= low, 1, 0)
        within = within + jnp.where(start <= high, 1, 0)
    lane = lax.broadcasted_iota(jnp.int32, (PIECE, 128), 1)
    row = lax.broadcasted_iota(jnp.int32, (PIECE, 128), 0)
    unit, offset = jnp.where(lane == 0, 1, 0), jnp.where(lane == 1, row, 0)
    beside = jnp.where(lane == 1, 1, 0)
    nexts = [jnp.int32(0), below, within]
    for ref, at, start, shift in pieces:
        first, second = start <= low, start <= high
        to = jnp.where(first, nexts[0], jnp.where(second, nexts[1], nexts[2]))
        nexts[0] = nexts[0] + jnp.where(first, 1, 0)
        nexts[1] = nexts[1] + jnp.where(second & (start > low), 1, 0)
        nexts[2] = nexts[2] + jnp.where(second, 0, 1)
        to = pl.ds(pl.multiple_of(to * PIECE, PIECE), PIECE)
        keys[to, :] = ref[at]
        mark = unit * (start // block) + offset + beside * shift
        marks[to, :] = mark.astype(jnp.float32).astype(jnp.bfloat16)

    read = jnp.where(lane == 0, float(block), jnp.where(lane == 1, 1.0, 0.0)).astype(jnp.bfloat16)
    query_row = lax.broadcasted_iota(jnp.int32, (block, TILE), 0).astype(jnp.float32)
    per_tile = TILE // PIECE
    tiles_low = (below + per_tile - 1) // per_tile
    tiles = tiles_low + (within + per_tile - 1) // per_tile

    def place(index):
        is_high = index >= tiles_low
        half = jnp.where(is_high, 1, 0)
        at = jnp.minimum((index - half * tiles_low) * TILE, keys.shape[0] - TILE)
        start = jnp.where(index >= tiles, -block, jnp.where(is_high, high, low))
        return half, pl.multiple_of(at, TILE), start

    def score(buffer, index):
        half, at, start = place(index)
        position = lax.dot_general(
            read,
            marks[pl.ds(at, TILE), :],
            (((1,), (1,)), ((), ())),
            preferred_element_type=jnp.float32,
        )
        position = jnp.broadcast_to(position[:1, :], (block, TILE))
        allowed = position - start.astype(jnp.float32) <= query_row
        s = lax.dot_general(
            query_ref[half],
            keys[pl.ds(at, TILE), :],
            (((1,), (1,)), ((), ())),
            preferred_element_type=jnp.float32,
        )
        s = jnp.where(allowed[None], s.reshape(rows // block, block, TILE), -1e30)
        buffer[...] = s.reshape(rows, TILE)

    def absorb_tile(buffer, index):
        half, at, _ = place(index)
        own = pl.ds(pl.multiple_of(half * rows, rows), rows)
        left, right = buffer[:, :128], buffer[:, 128:]
        old = top[own, :]
        new = jnp.maximum(old, jnp.max(jnp.maximum(left, right), axis=1, keepdims=True))
        scale = jnp.exp2((old - new) * factor)
        left = jnp.exp2((left - new) * factor)
        right = jnp.exp2((right - new) * factor)
        top[own, :] = new
        total[own, :] = total[own, :] * scale + (left + right)
        weights = jnp.concatenate([left, right], axis=1).astype(jnp.bfloat16)
        scales = jnp.concatenate([scale] * (latent_width // 128), axis=1)
        acc[own, :] = acc[own, :] * scales + jnp.dot(
            weights, keys[pl.ds(at, TILE), :latent_width], preferred_element_type=jnp.float32
        )

    score(even, 0)

    @pl.loop(0, (tiles + 1) // 2)
    def _(step):
        score(odd, 2 * step + 1)
        absorb_tile(even, 2 * step)
        score(even, 2 * step + 2)
        absorb_tile(odd, 2 * step + 1)

    if finish:
        value_width = uv_ref.shape[2]
        for h in range(uv_ref.shape[0]):
            lat = []
            for half in range(2):
                own = slice(half * rows + h * block, half * rows + (h + 1) * block)
                whole = jnp.sum(total[own, :], axis=1, keepdims=True)
                lat.append((acc[own, :] / whole).astype(jnp.bfloat16))
            out_ref[:, h * value_width : (h + 1) * value_width] = jnp.dot(
                jnp.concatenate(lat), uv_ref[h], preferred_element_type=jnp.float32
            ).astype(jnp.bfloat16)


def absorb(lasts, finish, block_start, query, pieces, state, w_uv):
    heads, latent_width, value_width = w_uv.shape
    rows, width = query.shape[1:]
    count = sum(p.shape[0] * p.shape[1] for p in pieces)
    vmem = pl.BlockSpec(memory_space=pltpu.VMEM)
    state_shapes = [(2 * rows, latent_width), (2 * rows, 128), (2 * rows, 128)]
    scratch = [
        pltpu.VMEM((count, width), jnp.bfloat16),
        pltpu.VMEM((count, 128), jnp.bfloat16),
        pltpu.VMEM((rows, TILE), jnp.float32),
        pltpu.VMEM((rows, TILE), jnp.float32),
    ]
    operands = [block_start, query, *pieces, *state]
    if finish:
        operands.append(w_uv)
        scratch += [pltpu.VMEM(shape, jnp.float32) for shape in state_shapes]
        out_shape = jax.ShapeDtypeStruct((2 * rows // heads, heads * value_width), jnp.bfloat16)
    else:
        out_shape = [jax.ShapeDtypeStruct(shape, jnp.float32) for shape in state_shapes]
    return pl.pallas_call(
        functools.partial(absorb_kernel, lasts, finish),
        in_specs=[pl.BlockSpec(memory_space=pltpu.SMEM)] + [vmem] * (len(operands) - 1),
        out_specs=vmem if finish else [vmem] * 3,
        out_shape=out_shape,
        scratch_shapes=scratch,
        compiler_params=pltpu.CompilerParams(vmem_limit_bytes=24 * 2**20),
        cost_estimate=pl.CostEstimate(
            flops=2 * rows * count * (width + latent_width),
            bytes_accessed=10 * 2**20,
            transcendentals=rows * count,
        ),
        name=f"absorb_{lasts[0]}",
    )(*operands)


def shards(q_nope, q_rope, latent, block_start, w_uk, w_uv):
    query = make_queries(q_nope, q_rope, w_uk)
    own, query = gather_own_core(latent, query)
    state = ()
    for lasts in GROUPS:
        chunks = [own[last] for last in lasts]
        if state:
            *chunks, state = lax.optimization_barrier((*chunks, state))
        pieces = [piece for chunk in chunks for piece in (chunk, other_core(chunk))]
        finish = lasts[-1] == len(own) - 1
        state = absorb(lasts, finish, block_start, query, pieces, state, w_uv)
    return state


def solution(mesh):
    placed = (P("ctx", "head"), P("ctx", "head"), P(BOTH, None), P(), P("head"), P("head"))
    return jax.shard_map(
        shards, mesh=mesh, in_specs=placed, out_specs=P("ctx", "head"), check_vma=False
    )
```

```python
import functools
import math

import jax
import jax.numpy as jnp
from jax import lax
from jax.experimental import pallas as pl
from jax.experimental.pallas import tpu as pltpu
from jax.sharding import PartitionSpec as P

BOTH = ("ctx", "head")
PIECE = 16
TILE = 256
NOPE = 128
GROUPS = ((0,), (1, 2, 3))
OFFSETS = (0, 1, 3, 2)
WINDOW = (0, 1, 7, 3, 4, 2, 5, 6)


def device_index(x, y, z, core):
    return (((x % 2) * 8 + z) * 2 + core) * 8 + (x // 2) * 4 + y


def from_offset(value, first, second):
    pairs = []
    for x in range(4):
        for y in range(4):
            for z in range(8):
                for core in range(2):
                    dx, dy, dz = second if core else first
                    source = device_index((x + dx) % 4, (y + dy) % 4, (z + dz) % 8, core)
                    pairs.append((source, device_index(x, y, z, core)))
    return lax.ppermute(value, BOTH, pairs)


def other_core(value):
    return lax.ppermute(value, "ctx", [(i, i ^ 1) for i in range(32)])


def gather_own_core(latent, query):
    latent = latent[None]
    up = from_offset(latent, (0, 0, 1), (0, 0, 1))
    down = from_offset(latent, (0, 0, 7), (0, 0, 7))
    window = jnp.concatenate([latent, up, down])
    far_up = from_offset(window, (0, 0, 3), (0, 0, 3))
    far_down = from_offset(window, (0, 0, 5), (0, 0, 5))[:2]
    column = jnp.concatenate([window, far_up, far_down])
    column, query = lax.optimization_barrier((column, query))
    plane = jnp.concatenate(
        [column] + [from_offset(column, (0, d, 0), (d, 0, 0)) for d in OFFSETS[1:]]
    )
    lines = [from_offset(plane, (d, 0, 0), (0, d, 0)) for d in OFFSETS[1:]]
    return [plane, *lines], query


def query_kernel(nope_ref, rope_ref, uk_ref, query_ref):
    latent_width = uk_ref.shape[2]
    nope_width = uk_ref.shape[1]
    rope_width = rope_ref.shape[1] // uk_ref.shape[0]
    block = nope_ref.shape[0] // 2
    for head in range(uk_ref.shape[0]):
        lat = jnp.dot(
            nope_ref[:, head * nope_width : (head + 1) * nope_width],
            uk_ref[head],
            preferred_element_type=jnp.float32,
        ).astype(jnp.bfloat16)
        rope = rope_ref[:, head * rope_width : (head + 1) * rope_width]
        for half in range(2):
            rows = slice(half * block, (half + 1) * block)
            to = slice(head * block, (head + 1) * block)
            query_ref[half, to, :latent_width] = lat[rows]
            query_ref[half, to, latent_width:] = rope[rows]


def make_queries(q_nope, q_rope, w_uk):
    rows = q_nope.shape[0]
    heads, nope_width, latent_width = w_uk.shape
    rope_width = q_rope.shape[1] // heads
    width = latent_width + rope_width
    vmem = pl.BlockSpec(memory_space=pltpu.VMEM)
    return pl.pallas_call(
        query_kernel,
        in_specs=[vmem] * 3,
        out_specs=vmem,
        out_shape=jax.ShapeDtypeStruct((2, heads * rows // 2, width), jnp.bfloat16),
        compiler_params=pltpu.CompilerParams(vmem_limit_bytes=12 * 2**20),
        cost_estimate=pl.CostEstimate(
            flops=2 * rows * heads * nope_width * latent_width,
            bytes_accessed=6 * 2**20,
            transcendentals=0,
        ),
        name="make_queries",
    )(q_nope, q_rope, w_uk)


def absorb_kernel(lasts, finish, starts_ref, query_ref, *refs):
    piece_refs, refs = refs[: 2 * len(lasts)], refs[2 * len(lasts) :]
    state_in = refs[: 0 if lasts[0] == 0 else 3]
    refs = refs[len(state_in) :]
    if finish:
        uv_ref, out_ref, keys, marks, even, odd, acc, top, total = refs
    else:
        acc, top, total, keys, marks, even, odd = refs
    ctx, head_group = lax.axis_index("ctx"), lax.axis_index("head")
    x = (head_group >> 2) * 2 + (ctx >> 4)
    y, z, core = head_group & 3, (ctx >> 1) & 7, ctx & 1
    rows = query_ref.shape[1]
    block, width = 4 * PIECE, query_ref.shape[2]
    latent_width = acc.shape[1]
    factor = math.log2(math.e) / math.sqrt(NOPE + width - latent_width)
    low, high = starts_ref[2 * ctx], starts_ref[2 * ctx + 1]

    if state_in:
        for to_ref, from_ref in zip((acc, top, total), state_in):
            to_ref[...] = from_ref[...]
    else:
        top[...] = jnp.full(top.shape, -1e30, jnp.float32)
        total[...] = jnp.zeros(total.shape, jnp.float32)
        acc[...] = jnp.zeros(acc.shape, jnp.float32)

    pieces = []
    for index, ref in enumerate(piece_refs):
        last, owner = lasts[index // 2], core if index % 2 == 0 else 1 - core
        for middle in range(4):
            px = (x + jnp.where(owner == 0, OFFSETS[last], OFFSETS[middle])) & 3
            py = (y + jnp.where(owner == 0, OFFSETS[middle], OFFSETS[last])) & 3
            for first in range(8):
                pz = (z + WINDOW[first]) & 7
                start = starts_ref[((px & 1) << 5) + (pz << 2) + (owner << 1) + (px >> 1)]
                pieces.append((ref, middle * 8 + first, start, py * PIECE))
    below = jnp.int32(0)
    within = jnp.int32(0)
    for _, _, start, _ in pieces:
        below = below + jnp.where(start <= low, 1, 0)
        within = within + jnp.where(start <= high, 1, 0)
    lane = lax.broadcasted_iota(jnp.int32, (PIECE, 128), 1)
    row = lax.broadcasted_iota(jnp.int32, (PIECE, 128), 0)
    unit, offset = jnp.where(lane == 0, 1, 0), jnp.where(lane == 1, row, 0)
    beside = jnp.where(lane == 1, 1, 0)
    nexts = [jnp.int32(0), below, within]
    for ref, at, start, shift in pieces:
        first, second = start <= low, start <= high
        to = jnp.where(first, nexts[0], jnp.where(second, nexts[1], nexts[2]))
        nexts[0] = nexts[0] + jnp.where(first, 1, 0)
        nexts[1] = nexts[1] + jnp.where(second & (start > low), 1, 0)
        nexts[2] = nexts[2] + jnp.where(second, 0, 1)
        to = pl.ds(pl.multiple_of(to * PIECE, PIECE), PIECE)
        keys[to, :] = ref[at]
        mark = unit * (start >> 6) + offset + beside * shift
        marks[to, :] = mark.astype(jnp.float32).astype(jnp.bfloat16)

    read = jnp.where(lane == 0, float(block), jnp.where(lane == 1, 1.0, 0.0)).astype(jnp.bfloat16)
    query_row = lax.broadcasted_iota(jnp.int32, (block, TILE), 0).astype(jnp.float32)
    per_tile = TILE // PIECE
    tiles_low = (below + per_tile - 1) >> 4
    tiles = tiles_low + ((within + per_tile - 1) >> 4)

    def place(index):
        is_high = index >= tiles_low
        half = jnp.where(is_high, 1, 0)
        at = jnp.minimum((index - half * tiles_low) * TILE, keys.shape[0] - TILE)
        start = jnp.where(index >= tiles, -block, jnp.where(is_high, high, low))
        return half, pl.multiple_of(at, TILE), start

    def score(buffer, index):
        half, at, start = place(index)
        position = lax.dot_general(
            read,
            marks[pl.ds(at, TILE), :],
            (((1,), (1,)), ((), ())),
            preferred_element_type=jnp.float32,
        )
        position = jnp.broadcast_to(position[:1, :], (block, TILE))
        allowed = position - start.astype(jnp.float32) <= query_row
        s = lax.dot_general(
            query_ref[half],
            keys[pl.ds(at, TILE), :],
            (((1,), (1,)), ((), ())),
            preferred_element_type=jnp.float32,
        )
        s = jnp.where(allowed[None], s.reshape(rows // block, block, TILE), -1e30)
        buffer[...] = s.reshape(rows, TILE)

    def absorb_tile(buffer, index):
        half, at, _ = place(index)
        own = pl.ds(pl.multiple_of(half * rows, rows), rows)
        left, right = buffer[:, :128], buffer[:, 128:]
        old = top[own, :]
        new = jnp.maximum(old, jnp.max(jnp.maximum(left, right), axis=1, keepdims=True))
        scale = jnp.exp2((old - new) * factor)
        left = jnp.exp2((left - new) * factor)
        right = jnp.exp2((right - new) * factor)
        top[own, :] = new
        total[own, :] = total[own, :] * scale + (left + right)
        weights = jnp.concatenate([left, right], axis=1).astype(jnp.bfloat16)
        scales = jnp.concatenate([scale] * (latent_width // 128), axis=1)
        acc[own, :] = acc[own, :] * scales + jnp.dot(
            weights, keys[pl.ds(at, TILE), :latent_width], preferred_element_type=jnp.float32
        )

    score(even, 0)

    @pl.loop(0, (tiles + 1) >> 1)
    def _(step):
        score(odd, 2 * step + 1)
        absorb_tile(even, 2 * step)
        score(even, 2 * step + 2)
        absorb_tile(odd, 2 * step + 1)

    if finish:
        value_width = uv_ref.shape[2]
        for h in range(uv_ref.shape[0]):
            lat = []
            for half in range(2):
                own = slice(half * rows + h * block, half * rows + (h + 1) * block)
                whole = jnp.sum(total[own, :], axis=1, keepdims=True)
                lat.append((acc[own, :] / whole).astype(jnp.bfloat16))
            out_ref[:, h * value_width : (h + 1) * value_width] = jnp.dot(
                jnp.concatenate(lat), uv_ref[h], preferred_element_type=jnp.float32
            ).astype(jnp.bfloat16)


def absorb(lasts, finish, block_start, query, pieces, state, w_uv):
    heads, latent_width, value_width = w_uv.shape
    rows, width = query.shape[1:]
    count = sum(p.shape[0] * p.shape[1] for p in pieces)
    vmem = pl.BlockSpec(memory_space=pltpu.VMEM)
    state_shapes = [(2 * rows, latent_width), (2 * rows, 128), (2 * rows, 128)]
    scratch = [
        pltpu.VMEM((count, width), jnp.bfloat16),
        pltpu.VMEM((count, 128), jnp.bfloat16),
        pltpu.VMEM((rows, TILE), jnp.float32),
        pltpu.VMEM((rows, TILE), jnp.float32),
    ]
    operands = [block_start, query, *pieces, *state]
    if finish:
        operands.append(w_uv)
        scratch += [pltpu.VMEM(shape, jnp.float32) for shape in state_shapes]
        out_shape = jax.ShapeDtypeStruct((2 * rows // heads, heads * value_width), jnp.bfloat16)
    else:
        out_shape = [jax.ShapeDtypeStruct(shape, jnp.float32) for shape in state_shapes]
    return pl.pallas_call(
        functools.partial(absorb_kernel, lasts, finish),
        in_specs=[pl.BlockSpec(memory_space=pltpu.SMEM)] + [vmem] * (len(operands) - 1),
        out_specs=vmem if finish else [vmem] * 3,
        out_shape=out_shape,
        scratch_shapes=scratch,
        compiler_params=pltpu.CompilerParams(vmem_limit_bytes=24 * 2**20),
        cost_estimate=pl.CostEstimate(
            flops=2 * rows * count * (width + latent_width),
            bytes_accessed=10 * 2**20,
            transcendentals=rows * count,
        ),
        name=f"absorb_{lasts[0]}",
    )(*operands)


def shards(q_nope, q_rope, latent, block_start, w_uk, w_uv):
    query = make_queries(q_nope, q_rope, w_uk)
    own, query = gather_own_core(latent, query)
    state = ()
    for lasts in GROUPS:
        chunks = [own[last] for last in lasts]
        for i in range(len(chunks) if state else 0):
            chunks[i], state = lax.optimization_barrier((chunks[i], state))
        pieces = [piece for chunk in chunks for piece in (chunk, other_core(chunk))]
        finish = lasts[-1] == len(own) - 1
        state = absorb(lasts, finish, block_start, query, pieces, state, w_uv)
    return state


def solution(mesh):
    placed = (P("ctx", "head"), P("ctx", "head"), P(BOTH, None), P(), P("head"), P("head"))
    return jax.shard_map(
        shards, mesh=mesh, in_specs=placed, out_specs=P("ctx", "head"), check_vma=False
    )
```

```python
import functools
import math

import jax
import jax.numpy as jnp
from jax import lax
from jax.experimental import pallas as pl
from jax.experimental.pallas import tpu as pltpu
from jax.sharding import PartitionSpec as P

BOTH = ("ctx", "head")
PIECE = 16
TILE = 256
NOPE = 128
GROUPS = ((0,), (1, 2), (3,))
OFFSETS = (0, 1, 3, 2)
WINDOW = (0, 1, 7, 3, 4, 2, 5, 6)


def device_index(x, y, z, core):
    return (((x % 2) * 8 + z) * 2 + core) * 8 + (x // 2) * 4 + y


def from_offset(value, first, second):
    pairs = []
    for x in range(4):
        for y in range(4):
            for z in range(8):
                for core in range(2):
                    dx, dy, dz = second if core else first
                    source = device_index((x + dx) % 4, (y + dy) % 4, (z + dz) % 8, core)
                    pairs.append((source, device_index(x, y, z, core)))
    return lax.ppermute(value, BOTH, pairs)


def other_core(value):
    return lax.ppermute(value, "ctx", [(i, i ^ 1) for i in range(32)])


def gather_own_core(latent, query):
    latent = latent[None]
    up = from_offset(latent, (0, 0, 1), (0, 0, 1))
    down = from_offset(latent, (0, 0, 7), (0, 0, 7))
    window = jnp.concatenate([latent, up, down])
    far_up = from_offset(window, (0, 0, 3), (0, 0, 3))
    far_down = from_offset(window, (0, 0, 5), (0, 0, 5))[:2]
    column = jnp.concatenate([window, far_up, far_down])
    column, query = lax.optimization_barrier((column, query))
    plane = jnp.concatenate(
        [column] + [from_offset(column, (0, d, 0), (d, 0, 0)) for d in OFFSETS[1:]]
    )
    lines = [from_offset(plane, (d, 0, 0), (0, d, 0)) for d in OFFSETS[1:]]
    return [plane, *lines], query


def query_kernel(nope_ref, rope_ref, uk_ref, query_ref):
    latent_width = uk_ref.shape[2]
    nope_width = uk_ref.shape[1]
    rope_width = rope_ref.shape[1] // uk_ref.shape[0]
    block = nope_ref.shape[0] // 2
    for head in range(uk_ref.shape[0]):
        lat = jnp.dot(
            nope_ref[:, head * nope_width : (head + 1) * nope_width],
            uk_ref[head],
            preferred_element_type=jnp.float32,
        ).astype(jnp.bfloat16)
        rope = rope_ref[:, head * rope_width : (head + 1) * rope_width]
        for half in range(2):
            rows = slice(half * block, (half + 1) * block)
            to = slice(head * block, (head + 1) * block)
            query_ref[half, to, :latent_width] = lat[rows]
            query_ref[half, to, latent_width:] = rope[rows]


def make_queries(q_nope, q_rope, w_uk):
    rows = q_nope.shape[0]
    heads, nope_width, latent_width = w_uk.shape
    rope_width = q_rope.shape[1] // heads
    width = latent_width + rope_width
    vmem = pl.BlockSpec(memory_space=pltpu.VMEM)
    return pl.pallas_call(
        query_kernel,
        in_specs=[vmem] * 3,
        out_specs=vmem,
        out_shape=jax.ShapeDtypeStruct((2, heads * rows // 2, width), jnp.bfloat16),
        compiler_params=pltpu.CompilerParams(vmem_limit_bytes=12 * 2**20),
        cost_estimate=pl.CostEstimate(
            flops=2 * rows * heads * nope_width * latent_width,
            bytes_accessed=6 * 2**20,
            transcendentals=0,
        ),
        name="make_queries",
    )(q_nope, q_rope, w_uk)


def absorb_kernel(lasts, finish, starts_ref, query_ref, *refs):
    piece_refs, refs = refs[: 2 * len(lasts)], refs[2 * len(lasts) :]
    state_in = refs[: 0 if lasts[0] == 0 else 3]
    refs = refs[len(state_in) :]
    if finish:
        uv_ref, out_ref, keys, marks, even, odd, acc, top, total = refs
    else:
        acc, top, total, keys, marks, even, odd = refs
    ctx, head_group = lax.axis_index("ctx"), lax.axis_index("head")
    x = (head_group >> 2) * 2 + (ctx >> 4)
    y, z, core = head_group & 3, (ctx >> 1) & 7, ctx & 1
    rows = query_ref.shape[1]
    block, width = 4 * PIECE, query_ref.shape[2]
    latent_width = acc.shape[1]
    factor = math.log2(math.e) / math.sqrt(NOPE + width - latent_width)
    low, high = starts_ref[2 * ctx], starts_ref[2 * ctx + 1]

    if state_in:
        for to_ref, from_ref in zip((acc, top, total), state_in):
            to_ref[...] = from_ref[...]
    else:
        top[...] = jnp.full(top.shape, -1e30, jnp.float32)
        total[...] = jnp.zeros(total.shape, jnp.float32)
        acc[...] = jnp.zeros(acc.shape, jnp.float32)

    pieces = []
    for index, ref in enumerate(piece_refs):
        last, owner = lasts[index // 2], core if index % 2 == 0 else 1 - core
        for middle in range(4):
            px = (x + jnp.where(owner == 0, OFFSETS[last], OFFSETS[middle])) & 3
            py = (y + jnp.where(owner == 0, OFFSETS[middle], OFFSETS[last])) & 3
            for first in range(8):
                pz = (z + WINDOW[first]) & 7
                start = starts_ref[((px & 1) << 5) + (pz << 2) + (owner << 1) + (px >> 1)]
                pieces.append((ref, middle * 8 + first, start, py * PIECE))
    below = jnp.int32(0)
    within = jnp.int32(0)
    for _, _, start, _ in pieces:
        below = below + jnp.where(start <= low, 1, 0)
        within = within + jnp.where(start <= high, 1, 0)
    lane = lax.broadcasted_iota(jnp.int32, (PIECE, 128), 1)
    row = lax.broadcasted_iota(jnp.int32, (PIECE, 128), 0)
    unit, offset = jnp.where(lane == 0, 1, 0), jnp.where(lane == 1, row, 0)
    beside = jnp.where(lane == 1, 1, 0)
    nexts = [jnp.int32(0), below, within]
    for ref, at, start, shift in pieces:
        first, second = start <= low, start <= high
        to = jnp.where(first, nexts[0], jnp.where(second, nexts[1], nexts[2]))
        nexts[0] = nexts[0] + jnp.where(first, 1, 0)
        nexts[1] = nexts[1] + jnp.where(second & (start > low), 1, 0)
        nexts[2] = nexts[2] + jnp.where(second, 0, 1)
        to = pl.ds(pl.multiple_of(to * PIECE, PIECE), PIECE)
        keys[to, :] = ref[at]
        mark = unit * (start >> 6) + offset + beside * shift
        marks[to, :] = mark.astype(jnp.float32).astype(jnp.bfloat16)

    read = jnp.where(lane == 0, float(block), jnp.where(lane == 1, 1.0, 0.0)).astype(jnp.bfloat16)
    query_row = lax.broadcasted_iota(jnp.int32, (block, TILE), 0).astype(jnp.float32)
    per_tile = TILE // PIECE
    tiles_low = (below + per_tile - 1) >> 4
    tiles = tiles_low + ((within + per_tile - 1) >> 4)

    def place(index):
        is_high = index >= tiles_low
        half = jnp.where(is_high, 1, 0)
        at = jnp.minimum((index - half * tiles_low) * TILE, keys.shape[0] - TILE)
        start = jnp.where(is_high, high, low)
        return half, pl.multiple_of(at, TILE), start

    def score(buffer, index):
        half, at, start = place(index)
        position = lax.dot_general(
            read,
            marks[pl.ds(at, TILE), :],
            (((1,), (1,)), ((), ())),
            preferred_element_type=jnp.float32,
        )
        position = jnp.broadcast_to(position[:1, :], (block, TILE))
        allowed = position - start.astype(jnp.float32) <= query_row
        s = lax.dot_general(
            query_ref[half],
            keys[pl.ds(at, TILE), :],
            (((1,), (1,)), ((), ())),
            preferred_element_type=jnp.float32,
        )
        s = jnp.where(allowed[None], s.reshape(rows // block, block, TILE), -1e30)
        buffer[...] = s.reshape(rows, TILE)

    def absorb_tile(buffer, index):
        half, at, _ = place(index)
        own = pl.ds(pl.multiple_of(half * rows, rows), rows)
        left, right = buffer[:, :128], buffer[:, 128:]
        old = top[own, :]
        new = jnp.maximum(old, jnp.max(jnp.maximum(left, right), axis=1, keepdims=True))
        scale = jnp.exp2((old - new) * factor)
        left = jnp.exp2((left - new) * factor)
        right = jnp.exp2((right - new) * factor)
        top[own, :] = new
        total[own, :] = total[own, :] * scale + (left + right)
        weights = jnp.concatenate([left, right], axis=1).astype(jnp.bfloat16)
        scales = jnp.concatenate([scale] * (latent_width // 128), axis=1)
        acc[own, :] = acc[own, :] * scales + jnp.dot(
            weights, keys[pl.ds(at, TILE), :latent_width], preferred_element_type=jnp.float32
        )

    score(even, 0)

    @pl.loop(0, tiles - 1)
    def _(index):
        @pl.when((index & 1) == 0)
        def _():
            score(odd, index + 1)
            absorb_tile(even, index)

        @pl.when((index & 1) == 1)
        def _():
            score(even, index + 1)
            absorb_tile(odd, index)

    @pl.when((tiles & 1) == 1)
    def _():
        absorb_tile(even, tiles - 1)

    @pl.when((tiles & 1) == 0)
    def _():
        absorb_tile(odd, tiles - 1)

    if finish:
        value_width = uv_ref.shape[2]
        for h in range(uv_ref.shape[0]):
            lat = []
            for half in range(2):
                own = slice(half * rows + h * block, half * rows + (h + 1) * block)
                whole = jnp.sum(total[own, :], axis=1, keepdims=True)
                lat.append((acc[own, :] / whole).astype(jnp.bfloat16))
            out_ref[:, h * value_width : (h + 1) * value_width] = jnp.dot(
                jnp.concatenate(lat), uv_ref[h], preferred_element_type=jnp.float32
            ).astype(jnp.bfloat16)


def absorb(lasts, finish, block_start, query, pieces, state, w_uv):
    heads, latent_width, value_width = w_uv.shape
    rows, width = query.shape[1:]
    count = sum(p.shape[0] * p.shape[1] for p in pieces)
    vmem = pl.BlockSpec(memory_space=pltpu.VMEM)
    state_shapes = [(2 * rows, latent_width), (2 * rows, 128), (2 * rows, 128)]
    scratch = [
        pltpu.VMEM((count, width), jnp.bfloat16),
        pltpu.VMEM((count, 128), jnp.bfloat16),
        pltpu.VMEM((rows, TILE), jnp.float32),
        pltpu.VMEM((rows, TILE), jnp.float32),
    ]
    operands = [block_start, query, *pieces, *state]
    if finish:
        operands.append(w_uv)
        scratch += [pltpu.VMEM(shape, jnp.float32) for shape in state_shapes]
        out_shape = jax.ShapeDtypeStruct((2 * rows // heads, heads * value_width), jnp.bfloat16)
    else:
        out_shape = [jax.ShapeDtypeStruct(shape, jnp.float32) for shape in state_shapes]
    return pl.pallas_call(
        functools.partial(absorb_kernel, lasts, finish),
        in_specs=[pl.BlockSpec(memory_space=pltpu.SMEM)] + [vmem] * (len(operands) - 1),
        out_specs=vmem if finish else [vmem] * 3,
        out_shape=out_shape,
        scratch_shapes=scratch,
        compiler_params=pltpu.CompilerParams(vmem_limit_bytes=24 * 2**20),
        cost_estimate=pl.CostEstimate(
            flops=2 * rows * count * (width + latent_width),
            bytes_accessed=10 * 2**20,
            transcendentals=rows * count,
        ),
        name=f"absorb_{lasts[0]}",
    )(*operands)


def shards(q_nope, q_rope, latent, block_start, w_uk, w_uv):
    query = make_queries(q_nope, q_rope, w_uk)
    own, query = gather_own_core(latent, query)
    state = ()
    for lasts in GROUPS:
        chunks = [own[last] for last in lasts]
        if state:
            *chunks, state = lax.optimization_barrier((*chunks, state))
        pieces = [piece for chunk in chunks for piece in (chunk, other_core(chunk))]
        finish = lasts[-1] == len(own) - 1
        state = absorb(lasts, finish, block_start, query, pieces, state, w_uv)
    return state


def solution(mesh):
    placed = (P("ctx", "head"), P("ctx", "head"), P(BOTH, None), P(), P("head"), P("head"))
    return jax.shard_map(
        shards, mesh=mesh, in_specs=placed, out_specs=P("ctx", "head"), check_vma=False
    )
```

```python
import functools
import math

import jax
import jax.numpy as jnp
from jax import lax
from jax.experimental import pallas as pl
from jax.experimental.pallas import tpu as pltpu
from jax.sharding import PartitionSpec as P

BOTH = ("ctx", "head")
PIECE = 16
TILE = 256
NOPE = 128
GROUPS = ((0,), (1, 2), (3,))
OFFSETS = (0, 1, 3, 2)
WINDOW = (0, 1, 7, 3, 4, 2, 5, 6)


def device_index(x, y, z, core):
    return (((x % 2) * 8 + z) * 2 + core) * 8 + (x // 2) * 4 + y


def from_offset(value, first, second):
    pairs = []
    for x in range(4):
        for y in range(4):
            for z in range(8):
                for core in range(2):
                    dx, dy, dz = second if core else first
                    source = device_index((x + dx) % 4, (y + dy) % 4, (z + dz) % 8, core)
                    pairs.append((source, device_index(x, y, z, core)))
    return lax.ppermute(value, BOTH, pairs)


def other_core(value):
    return lax.ppermute(value, "ctx", [(i, i ^ 1) for i in range(32)])


def gather_own_core(latent, query):
    latent = latent[None]
    up = from_offset(latent, (0, 0, 1), (0, 0, 1))
    down = from_offset(latent, (0, 0, 7), (0, 0, 7))
    window = jnp.concatenate([latent, up, down])
    far_up = from_offset(window, (0, 0, 3), (0, 0, 3))
    far_down = from_offset(window, (0, 0, 5), (0, 0, 5))[:2]
    column = jnp.concatenate([window, far_up, far_down])
    lines = [from_offset(column, (0, d, 0), (d, 0, 0)) for d in OFFSETS[1:]]
    *lines, query = lax.optimization_barrier((*lines, query))
    plane = jnp.concatenate([column, *lines])
    lines = [from_offset(plane, (d, 0, 0), (0, d, 0)) for d in OFFSETS[1:]]
    return [plane, *lines], query


def query_kernel(nope_ref, rope_ref, uk_ref, query_ref):
    latent_width = uk_ref.shape[2]
    nope_width = uk_ref.shape[1]
    rope_width = rope_ref.shape[1] // uk_ref.shape[0]
    block = nope_ref.shape[0] // 2
    for head in range(uk_ref.shape[0]):
        lat = jnp.dot(
            nope_ref[:, head * nope_width : (head + 1) * nope_width],
            uk_ref[head],
            preferred_element_type=jnp.float32,
        ).astype(jnp.bfloat16)
        rope = rope_ref[:, head * rope_width : (head + 1) * rope_width]
        for half in range(2):
            rows = slice(half * block, (half + 1) * block)
            to = slice(head * block, (head + 1) * block)
            query_ref[half, to, :latent_width] = lat[rows]
            query_ref[half, to, latent_width:] = rope[rows]


def make_queries(q_nope, q_rope, w_uk):
    rows = q_nope.shape[0]
    heads, nope_width, latent_width = w_uk.shape
    rope_width = q_rope.shape[1] // heads
    width = latent_width + rope_width
    vmem = pl.BlockSpec(memory_space=pltpu.VMEM)
    return pl.pallas_call(
        query_kernel,
        in_specs=[vmem] * 3,
        out_specs=vmem,
        out_shape=jax.ShapeDtypeStruct((2, heads * rows // 2, width), jnp.bfloat16),
        compiler_params=pltpu.CompilerParams(vmem_limit_bytes=12 * 2**20),
        cost_estimate=pl.CostEstimate(
            flops=2 * rows * heads * nope_width * latent_width,
            bytes_accessed=6 * 2**20,
            transcendentals=0,
        ),
        name="make_queries",
    )(q_nope, q_rope, w_uk)


def absorb_kernel(lasts, finish, starts_ref, query_ref, *refs):
    piece_refs, refs = refs[: 2 * len(lasts)], refs[2 * len(lasts) :]
    state_in = refs[: 0 if lasts[0] == 0 else 3]
    refs = refs[len(state_in) :]
    if finish:
        uv_ref, out_ref, keys, marks, even, odd, acc, top, total = refs
    else:
        acc, top, total, keys, marks, even, odd = refs
    ctx, head_group = lax.axis_index("ctx"), lax.axis_index("head")
    x = (head_group >> 2) * 2 + (ctx >> 4)
    y, z, core = head_group & 3, (ctx >> 1) & 7, ctx & 1
    rows = query_ref.shape[1]
    block, width = 4 * PIECE, query_ref.shape[2]
    latent_width = acc.shape[1]
    factor = math.log2(math.e) / math.sqrt(NOPE + width - latent_width)
    low, high = starts_ref[2 * ctx], starts_ref[2 * ctx + 1]

    if state_in:
        for to_ref, from_ref in zip((acc, top, total), state_in):
            to_ref[...] = from_ref[...]
    else:
        top[...] = jnp.full(top.shape, -1e30, jnp.float32)
        total[...] = jnp.zeros(total.shape, jnp.float32)
        acc[...] = jnp.zeros(acc.shape, jnp.float32)

    pieces = []
    for index, ref in enumerate(piece_refs):
        last, owner = lasts[index // 2], core if index % 2 == 0 else 1 - core
        for middle in range(4):
            px = (x + jnp.where(owner == 0, OFFSETS[last], OFFSETS[middle])) & 3
            py = (y + jnp.where(owner == 0, OFFSETS[middle], OFFSETS[last])) & 3
            for first in range(8):
                pz = (z + WINDOW[first]) & 7
                start = starts_ref[((px & 1) << 5) + (pz << 2) + (owner << 1) + (px >> 1)]
                pieces.append((ref, middle * 8 + first, start, py * PIECE))
    below = jnp.int32(0)
    within = jnp.int32(0)
    for _, _, start, _ in pieces:
        below = below + jnp.where(start <= low, 1, 0)
        within = within + jnp.where(start <= high, 1, 0)
    lane = lax.broadcasted_iota(jnp.int32, (PIECE, 128), 1)
    row = lax.broadcasted_iota(jnp.int32, (PIECE, 128), 0)
    unit, offset = jnp.where(lane == 0, 1, 0), jnp.where(lane == 1, row, 0)
    beside = jnp.where(lane == 1, 1, 0)
    nexts = [jnp.int32(0), below, within]
    for ref, at, start, shift in pieces:
        first, second = start <= low, start <= high
        to = jnp.where(first, nexts[0], jnp.where(second, nexts[1], nexts[2]))
        nexts[0] = nexts[0] + jnp.where(first, 1, 0)
        nexts[1] = nexts[1] + jnp.where(second & (start > low), 1, 0)
        nexts[2] = nexts[2] + jnp.where(second, 0, 1)
        to = pl.ds(pl.multiple_of(to * PIECE, PIECE), PIECE)
        keys[to, :] = ref[at]
        mark = unit * (start >> 6) + offset + beside * shift
        marks[to, :] = mark.astype(jnp.float32).astype(jnp.bfloat16)

    read = jnp.where(lane == 0, float(block), jnp.where(lane == 1, 1.0, 0.0)).astype(jnp.bfloat16)
    query_row = lax.broadcasted_iota(jnp.int32, (block, TILE), 0).astype(jnp.float32)
    per_tile = TILE // PIECE
    tiles_low = (below + per_tile - 1) >> 4
    tiles = tiles_low + ((within + per_tile - 1) >> 4)

    def place(index):
        is_high = index >= tiles_low
        half = jnp.where(is_high, 1, 0)
        at = jnp.minimum((index - half * tiles_low) * TILE, keys.shape[0] - TILE)
        start = jnp.where(is_high, high, low)
        return half, pl.multiple_of(at, TILE), start

    def score(buffer, index):
        half, at, start = place(index)
        position = lax.dot_general(
            read,
            marks[pl.ds(at, TILE), :],
            (((1,), (1,)), ((), ())),
            preferred_element_type=jnp.float32,
        )
        position = jnp.broadcast_to(position[:1, :], (block, TILE))
        allowed = position - start.astype(jnp.float32) <= query_row
        s = lax.dot_general(
            query_ref[half],
            keys[pl.ds(at, TILE), :],
            (((1,), (1,)), ((), ())),
            preferred_element_type=jnp.float32,
        )
        s = jnp.where(allowed[None], s.reshape(rows // block, block, TILE), -1e30)
        buffer[...] = s.reshape(rows, TILE)

    def absorb_tile(buffer, index):
        half, at, _ = place(index)
        own = pl.ds(pl.multiple_of(half * rows, rows), rows)
        left, right = buffer[:, :128], buffer[:, 128:]
        old = top[own, :]
        new = jnp.maximum(old, jnp.max(jnp.maximum(left, right), axis=1, keepdims=True))
        scale = jnp.exp2((old - new) * factor)
        left = jnp.exp2((left - new) * factor)
        right = jnp.exp2((right - new) * factor)
        top[own, :] = new
        total[own, :] = total[own, :] * scale + (left + right)
        weights = jnp.concatenate([left, right], axis=1).astype(jnp.bfloat16)
        scales = jnp.concatenate([scale] * (latent_width // 128), axis=1)
        acc[own, :] = acc[own, :] * scales + jnp.dot(
            weights, keys[pl.ds(at, TILE), :latent_width], preferred_element_type=jnp.float32
        )

    score(even, 0)

    @pl.loop(0, tiles - 1)
    def _(index):
        @pl.when((index & 1) == 0)
        def _():
            score(odd, index + 1)
            absorb_tile(even, index)

        @pl.when((index & 1) == 1)
        def _():
            score(even, index + 1)
            absorb_tile(odd, index)

    @pl.when((tiles & 1) == 1)
    def _():
        absorb_tile(even, tiles - 1)

    @pl.when((tiles & 1) == 0)
    def _():
        absorb_tile(odd, tiles - 1)

    if finish:
        value_width = uv_ref.shape[2]
        for h in range(uv_ref.shape[0]):
            lat = []
            for half in range(2):
                own = slice(half * rows + h * block, half * rows + (h + 1) * block)
                whole = jnp.sum(total[own, :], axis=1, keepdims=True)
                lat.append((acc[own, :] / whole).astype(jnp.bfloat16))
            out_ref[:, h * value_width : (h + 1) * value_width] = jnp.dot(
                jnp.concatenate(lat), uv_ref[h], preferred_element_type=jnp.float32
            ).astype(jnp.bfloat16)


def absorb(lasts, finish, block_start, query, pieces, state, w_uv):
    heads, latent_width, value_width = w_uv.shape
    rows, width = query.shape[1:]
    count = sum(p.shape[0] * p.shape[1] for p in pieces)
    vmem = pl.BlockSpec(memory_space=pltpu.VMEM)
    state_shapes = [(2 * rows, latent_width), (2 * rows, 128), (2 * rows, 128)]
    scratch = [
        pltpu.VMEM((count, width), jnp.bfloat16),
        pltpu.VMEM((count, 128), jnp.bfloat16),
        pltpu.VMEM((rows, TILE), jnp.float32),
        pltpu.VMEM((rows, TILE), jnp.float32),
    ]
    operands = [block_start, query, *pieces, *state]
    if finish:
        operands.append(w_uv)
        scratch += [pltpu.VMEM(shape, jnp.float32) for shape in state_shapes]
        out_shape = jax.ShapeDtypeStruct((2 * rows // heads, heads * value_width), jnp.bfloat16)
    else:
        out_shape = [jax.ShapeDtypeStruct(shape, jnp.float32) for shape in state_shapes]
    return pl.pallas_call(
        functools.partial(absorb_kernel, lasts, finish),
        in_specs=[pl.BlockSpec(memory_space=pltpu.SMEM)] + [vmem] * (len(operands) - 1),
        out_specs=vmem if finish else [vmem] * 3,
        out_shape=out_shape,
        scratch_shapes=scratch,
        compiler_params=pltpu.CompilerParams(vmem_limit_bytes=24 * 2**20),
        cost_estimate=pl.CostEstimate(
            flops=2 * rows * count * (width + latent_width),
            bytes_accessed=10 * 2**20,
            transcendentals=rows * count,
        ),
        name=f"absorb_{lasts[0]}",
    )(*operands)


def shards(q_nope, q_rope, latent, block_start, w_uk, w_uv):
    query = make_queries(q_nope, q_rope, w_uk)
    own, query = gather_own_core(latent, query)
    state = ()
    for lasts in GROUPS:
        chunks = [own[last] for last in lasts]
        if state:
            *chunks, state = lax.optimization_barrier((*chunks, state))
        pieces = [piece for chunk in chunks for piece in (chunk, other_core(chunk))]
        finish = lasts[-1] == len(own) - 1
        state = absorb(lasts, finish, block_start, query, pieces, state, w_uv)
    return state


def solution(mesh):
    placed = (P("ctx", "head"), P("ctx", "head"), P(BOTH, None), P(), P("head"), P("head"))
    return jax.shard_map(
        shards, mesh=mesh, in_specs=placed, out_specs=P("ctx", "head"), check_vma=False
    )
```

```python
import functools
import math

import jax
import jax.numpy as jnp
from jax import lax
from jax.experimental import pallas as pl
from jax.experimental.pallas import tpu as pltpu
from jax.sharding import PartitionSpec as P

BOTH = ("ctx", "head")
PIECE = 16
TILE = 256
NOPE = 128
GROUPS = (((0, 0),), ((1, 0), (2, 0), (0, 1)), ((3, 0), (1, 1), (2, 1)), ((3, 1),))
OFFSETS = (0, 1, 3, 2)
WINDOW = (0, 1, 7, 3, 4, 2, 5, 6)


def device_index(x, y, z, core):
    return (((x % 2) * 8 + z) * 2 + core) * 8 + (x // 2) * 4 + y


def from_offset(value, first, second):
    pairs = []
    for x in range(4):
        for y in range(4):
            for z in range(8):
                for core in range(2):
                    dx, dy, dz = second if core else first
                    source = device_index((x + dx) % 4, (y + dy) % 4, (z + dz) % 8, core)
                    pairs.append((source, device_index(x, y, z, core)))
    return lax.ppermute(value, BOTH, pairs)


def other_core(value):
    return lax.ppermute(value, "ctx", [(i, i ^ 1) for i in range(32)])


def gather_own_core(latent, query):
    latent = latent[None]
    up = from_offset(latent, (0, 0, 1), (0, 0, 1))
    down = from_offset(latent, (0, 0, 7), (0, 0, 7))
    window = jnp.concatenate([latent, up, down])
    far_up = from_offset(window, (0, 0, 3), (0, 0, 3))
    far_down = from_offset(window, (0, 0, 5), (0, 0, 5))[:2]
    column = jnp.concatenate([window, far_up, far_down])
    lines = [from_offset(column, (0, d, 0), (d, 0, 0)) for d in OFFSETS[1:]]
    *lines, query = lax.optimization_barrier((*lines, query))
    plane = jnp.concatenate([column, *lines])
    lines = [from_offset(plane, (d, 0, 0), (0, d, 0)) for d in OFFSETS[1:3]]
    return [plane, *lines], query


def query_kernel(nope_ref, rope_ref, uk_ref, query_ref):
    latent_width = uk_ref.shape[2]
    nope_width = uk_ref.shape[1]
    rope_width = rope_ref.shape[1] // uk_ref.shape[0]
    block = nope_ref.shape[0] // 2
    for head in range(uk_ref.shape[0]):
        lat = jnp.dot(
            nope_ref[:, head * nope_width : (head + 1) * nope_width],
            uk_ref[head],
            preferred_element_type=jnp.float32,
        ).astype(jnp.bfloat16)
        rope = rope_ref[:, head * rope_width : (head + 1) * rope_width]
        for half in range(2):
            rows = slice(half * block, (half + 1) * block)
            to = slice(head * block, (head + 1) * block)
            query_ref[half, to, :latent_width] = lat[rows]
            query_ref[half, to, latent_width:] = rope[rows]


def make_queries(q_nope, q_rope, w_uk):
    rows = q_nope.shape[0]
    heads, nope_width, latent_width = w_uk.shape
    rope_width = q_rope.shape[1] // heads
    width = latent_width + rope_width
    vmem = pl.BlockSpec(memory_space=pltpu.VMEM)
    return pl.pallas_call(
        query_kernel,
        in_specs=[vmem] * 3,
        out_specs=vmem,
        out_shape=jax.ShapeDtypeStruct((2, heads * rows // 2, width), jnp.bfloat16),
        compiler_params=pltpu.CompilerParams(vmem_limit_bytes=12 * 2**20),
        cost_estimate=pl.CostEstimate(
            flops=2 * rows * heads * nope_width * latent_width,
            bytes_accessed=6 * 2**20,
            transcendentals=0,
        ),
        name="make_queries",
    )(q_nope, q_rope, w_uk)


def absorb_kernel(group, finish, starts_ref, query_ref, *refs):
    piece_refs, refs = refs[: len(group)], refs[len(group) :]
    state_in = refs[: 0 if group == GROUPS[0] else 3]
    refs = refs[len(state_in) :]
    if finish:
        uv_ref, out_ref, keys, marks, even, odd, acc, top, total = refs
    else:
        acc, top, total, keys, marks, even, odd = refs
    ctx, head_group = lax.axis_index("ctx"), lax.axis_index("head")
    x = (head_group >> 2) * 2 + (ctx >> 4)
    y, z, core = head_group & 3, (ctx >> 1) & 7, ctx & 1
    rows = query_ref.shape[1]
    block, width = 4 * PIECE, query_ref.shape[2]
    latent_width = acc.shape[1]
    factor = math.log2(math.e) / math.sqrt(NOPE + width - latent_width)
    low, high = starts_ref[2 * ctx], starts_ref[2 * ctx + 1]

    if state_in:
        for to_ref, from_ref in zip((acc, top, total), state_in):
            to_ref[...] = from_ref[...]
    else:
        top[...] = jnp.full(top.shape, -1e30, jnp.float32)
        total[...] = jnp.zeros(total.shape, jnp.float32)
        acc[...] = jnp.zeros(acc.shape, jnp.float32)

    pieces = []
    for index, ref in enumerate(piece_refs):
        last, side = group[index]
        owner = 1 - core if side else core
        for middle in range(4):
            px = (x + jnp.where(owner == 0, OFFSETS[last], OFFSETS[middle])) & 3
            py = (y + jnp.where(owner == 0, OFFSETS[middle], OFFSETS[last])) & 3
            for first in range(8):
                pz = (z + WINDOW[first]) & 7
                start = starts_ref[((px & 1) << 5) + (pz << 2) + (owner << 1) + (px >> 1)]
                pieces.append((ref, middle * 8 + first, start, py * PIECE))
    below = jnp.int32(0)
    within = jnp.int32(0)
    for _, _, start, _ in pieces:
        below = below + jnp.where(start <= low, 1, 0)
        within = within + jnp.where(start <= high, 1, 0)
    lane = lax.broadcasted_iota(jnp.int32, (PIECE, 128), 1)
    row = lax.broadcasted_iota(jnp.int32, (PIECE, 128), 0)
    unit, offset = jnp.where(lane == 0, 1, 0), jnp.where(lane == 1, row, 0)
    beside = jnp.where(lane == 1, 1, 0)
    nexts = [jnp.int32(0), below, within]
    for ref, at, start, shift in pieces:
        first, second = start <= low, start <= high
        to = jnp.where(first, nexts[0], jnp.where(second, nexts[1], nexts[2]))
        nexts[0] = nexts[0] + jnp.where(first, 1, 0)
        nexts[1] = nexts[1] + jnp.where(second & (start > low), 1, 0)
        nexts[2] = nexts[2] + jnp.where(second, 0, 1)
        to = pl.ds(pl.multiple_of(to * PIECE, PIECE), PIECE)
        keys[to, :] = ref[at]
        mark = unit * (start >> 6) + offset + beside * shift
        marks[to, :] = mark.astype(jnp.float32).astype(jnp.bfloat16)

    read = jnp.where(lane == 0, float(block), jnp.where(lane == 1, 1.0, 0.0)).astype(jnp.bfloat16)
    query_row = lax.broadcasted_iota(jnp.int32, (block, TILE), 0).astype(jnp.float32)
    per_tile = TILE // PIECE
    tiles_low = (below + per_tile - 1) >> 4
    tiles = tiles_low + ((within + per_tile - 1) >> 4)

    def place(index):
        is_high = index >= tiles_low
        half = jnp.where(is_high, 1, 0)
        at = jnp.minimum((index - half * tiles_low) * TILE, keys.shape[0] - TILE)
        start = jnp.where(is_high, high, low)
        return half, pl.multiple_of(at, TILE), start

    def score(buffer, index):
        half, at, start = place(index)
        position = lax.dot_general(
            read,
            marks[pl.ds(at, TILE), :],
            (((1,), (1,)), ((), ())),
            preferred_element_type=jnp.float32,
        )
        position = jnp.broadcast_to(position[:1, :], (block, TILE))
        allowed = position - start.astype(jnp.float32) <= query_row
        s = lax.dot_general(
            query_ref[half],
            keys[pl.ds(at, TILE), :],
            (((1,), (1,)), ((), ())),
            preferred_element_type=jnp.float32,
        )
        s = jnp.where(allowed[None], s.reshape(rows // block, block, TILE), -1e30)
        buffer[...] = s.reshape(rows, TILE)

    def absorb_tile(buffer, index):
        half, at, _ = place(index)
        own = pl.ds(pl.multiple_of(half * rows, rows), rows)
        left, right = buffer[:, :128], buffer[:, 128:]
        old = top[own, :]
        new = jnp.maximum(old, jnp.max(jnp.maximum(left, right), axis=1, keepdims=True))
        scale = jnp.exp2((old - new) * factor)
        left = jnp.exp2((left - new) * factor)
        right = jnp.exp2((right - new) * factor)
        top[own, :] = new
        total[own, :] = total[own, :] * scale + (left + right)
        weights = jnp.concatenate([left, right], axis=1).astype(jnp.bfloat16)
        scales = jnp.concatenate([scale] * (latent_width // 128), axis=1)
        acc[own, :] = acc[own, :] * scales + jnp.dot(
            weights, keys[pl.ds(at, TILE), :latent_width], preferred_element_type=jnp.float32
        )

    score(even, 0)

    @pl.loop(0, jnp.maximum(tiles - 1, 0))
    def _(index):
        @pl.when((index & 1) == 0)
        def _():
            score(odd, index + 1)
            absorb_tile(even, index)

        @pl.when((index & 1) == 1)
        def _():
            score(even, index + 1)
            absorb_tile(odd, index)

    @pl.when((tiles & 1) == 1)
    def _():
        absorb_tile(even, tiles - 1)

    @pl.when(((tiles & 1) == 0) & (tiles > 0))
    def _():
        absorb_tile(odd, tiles - 1)

    if finish:
        value_width = uv_ref.shape[2]
        for h in range(uv_ref.shape[0]):
            lat = []
            for half in range(2):
                own = slice(half * rows + h * block, half * rows + (h + 1) * block)
                whole = jnp.sum(total[own, :], axis=1, keepdims=True)
                lat.append((acc[own, :] / whole).astype(jnp.bfloat16))
            out_ref[:, h * value_width : (h + 1) * value_width] = jnp.dot(
                jnp.concatenate(lat), uv_ref[h], preferred_element_type=jnp.float32
            ).astype(jnp.bfloat16)


def absorb(group, finish, block_start, query, pieces, state, w_uv):
    heads, latent_width, value_width = w_uv.shape
    rows, width = query.shape[1:]
    count = sum(p.shape[0] * p.shape[1] for p in pieces)
    vmem = pl.BlockSpec(memory_space=pltpu.VMEM)
    state_shapes = [(2 * rows, latent_width), (2 * rows, 128), (2 * rows, 128)]
    scratch = [
        pltpu.VMEM((count, width), jnp.bfloat16),
        pltpu.VMEM((count, 128), jnp.bfloat16),
        pltpu.VMEM((rows, TILE), jnp.float32),
        pltpu.VMEM((rows, TILE), jnp.float32),
    ]
    operands = [block_start, query, *pieces, *state]
    if finish:
        operands.append(w_uv)
        scratch += [pltpu.VMEM(shape, jnp.float32) for shape in state_shapes]
        out_shape = jax.ShapeDtypeStruct((2 * rows // heads, heads * value_width), jnp.bfloat16)
    else:
        out_shape = [jax.ShapeDtypeStruct(shape, jnp.float32) for shape in state_shapes]
    return pl.pallas_call(
        functools.partial(absorb_kernel, group, finish),
        in_specs=[pl.BlockSpec(memory_space=pltpu.SMEM)] + [vmem] * (len(operands) - 1),
        out_specs=vmem if finish else [vmem] * 3,
        out_shape=out_shape,
        scratch_shapes=scratch,
        compiler_params=pltpu.CompilerParams(vmem_limit_bytes=24 * 2**20),
        cost_estimate=pl.CostEstimate(
            flops=4 * rows * count * (width + latent_width),
            bytes_accessed=10 * 2**20,
            transcendentals=rows * count,
        ),
        name=f"absorb_{GROUPS.index(group)}",
    )(*operands)


def shards(q_nope, q_rope, latent, block_start, w_uk, w_uv):
    query = make_queries(q_nope, q_rope, w_uk)
    own, query = gather_own_core(latent, query)
    state = ()
    for group in GROUPS:
        fresh = [last for last, side in group if side == 0]
        if state and fresh:
            *chunks, plane, state = lax.optimization_barrier(
                (*[own[last] for last in fresh], own[0], state)
            )
            for last, chunk in zip(fresh, chunks):
                own[last] = chunk
            if len(own) < len(OFFSETS):
                own.append(from_offset(plane, (OFFSETS[3], 0, 0), (0, OFFSETS[3], 0)))
        pieces = [other_core(own[last]) if side else own[last] for last, side in group]
        finish = group == GROUPS[-1]
        state = absorb(group, finish, block_start, query, pieces, state, w_uv)
    return state


def solution(mesh):
    placed = (P("ctx", "head"), P("ctx", "head"), P(BOTH, None), P(), P("head"), P("head"))
    return jax.shard_map(
        shards, mesh=mesh, in_specs=placed, out_specs=P("ctx", "head"), check_vma=False
    )
```

```python
import functools
import math

import jax
import jax.numpy as jnp
from jax import lax
from jax.experimental import pallas as pl
from jax.experimental.pallas import tpu as pltpu
from jax.sharding import PartitionSpec as P

BOTH = ("ctx", "head")
PIECE = 16
TILE = 256
NOPE = 128
GROUPS = ((0,), (1, 2), (3,))
OFFSETS = (0, 1, 3, 2)
WINDOW = (0, 1, 7, 3, 4, 2, 5, 6)


def device_index(x, y, z, core):
    return (((x % 2) * 8 + z) * 2 + core) * 8 + (x // 2) * 4 + y


def from_offset(value, first, second):
    pairs = []
    for x in range(4):
        for y in range(4):
            for z in range(8):
                for core in range(2):
                    dx, dy, dz = second if core else first
                    source = device_index((x + dx) % 4, (y + dy) % 4, (z + dz) % 8, core)
                    pairs.append((source, device_index(x, y, z, core)))
    return lax.ppermute(value, BOTH, pairs)


def other_core(value):
    return lax.ppermute(value, "ctx", [(i, i ^ 1) for i in range(32)])


def gather_own_core(latent, query):
    latent = latent[None]
    up = from_offset(latent, (0, 0, 1), (0, 0, 1))
    down = from_offset(latent, (0, 0, 7), (0, 0, 7))
    window = jnp.concatenate([latent, up, down])
    far_up = from_offset(window, (0, 0, 3), (0, 0, 3))
    far_down = from_offset(window, (0, 0, 5), (0, 0, 5))[:2]
    column = jnp.concatenate([window, far_up, far_down])
    lines = [from_offset(column, (0, d, 0), (d, 0, 0)) for d in OFFSETS[1:]]
    *lines, query = lax.optimization_barrier((*lines, query))
    plane = jnp.concatenate([column, *lines])
    lines = [from_offset(plane, (d, 0, 0), (0, d, 0)) for d in OFFSETS[1:]]
    return [plane, *lines], query


def query_kernel(nope_ref, rope_ref, uk_ref, query_ref):
    latent_width = uk_ref.shape[2]
    nope_width = uk_ref.shape[1]
    rope_width = rope_ref.shape[1] // uk_ref.shape[0]
    block = nope_ref.shape[0] // 2
    rest = jnp.zeros((block, query_ref.shape[2] - latent_width - rope_ref.shape[1] // uk_ref.shape[0]), jnp.bfloat16)
    lane = lax.broadcasted_iota(jnp.int32, (PIECE, 128), 1)
    read = jnp.where(lane == 64, float(block), jnp.where(lane == 65, 1.0, 0.0))
    for half in range(2):
        query_ref[half, :PIECE, :latent_width] = jnp.zeros((PIECE, latent_width), jnp.bfloat16)
        query_ref[half, :PIECE, latent_width:] = read.astype(jnp.bfloat16)
    for head in range(uk_ref.shape[0]):
        lat = jnp.dot(
            nope_ref[:, head * nope_width : (head + 1) * nope_width],
            uk_ref[head],
            preferred_element_type=jnp.float32,
        ).astype(jnp.bfloat16)
        rope = rope_ref[:, head * rope_width : (head + 1) * rope_width]
        for half in range(2):
            rows = slice(half * block, (half + 1) * block)
            to = slice(PIECE + head * block, PIECE + (head + 1) * block)
            query_ref[half, to, :latent_width] = lat[rows]
            query_ref[half, to, latent_width:] = jnp.concatenate([rope[rows], rest], axis=1)


def make_queries(q_nope, q_rope, w_uk):
    rows = q_nope.shape[0]
    heads, nope_width, latent_width = w_uk.shape
    rope_width = q_rope.shape[1] // heads
    width = latent_width + 2 * rope_width
    vmem = pl.BlockSpec(memory_space=pltpu.VMEM)
    return pl.pallas_call(
        query_kernel,
        in_specs=[vmem] * 3,
        out_specs=vmem,
        out_shape=jax.ShapeDtypeStruct((2, PIECE + heads * rows // 2, width), jnp.bfloat16),
        compiler_params=pltpu.CompilerParams(vmem_limit_bytes=12 * 2**20),
        cost_estimate=pl.CostEstimate(
            flops=2 * rows * heads * nope_width * latent_width,
            bytes_accessed=6 * 2**20,
            transcendentals=0,
        ),
        name="make_queries",
    )(q_nope, q_rope, w_uk)


def absorb_kernel(lasts, finish, starts_ref, query_ref, *refs):
    piece_refs, refs = refs[: 2 * len(lasts)], refs[2 * len(lasts) :]
    state_in = refs[: 0 if lasts[0] == 0 else 3]
    refs = refs[len(state_in) :]
    if finish:
        uv_ref, out_ref, keys, even, odd, acc, top, total = refs
    else:
        acc, top, total, keys, even, odd = refs
    ctx, head_group = lax.axis_index("ctx"), lax.axis_index("head")
    x = (head_group >> 2) * 2 + (ctx >> 4)
    y, z, core = head_group & 3, (ctx >> 1) & 7, ctx & 1
    rows = query_ref.shape[1] - PIECE
    block, width = 4 * PIECE, piece_refs[0].shape[2]
    latent_width = acc.shape[1]
    factor = math.log2(math.e) / math.sqrt(NOPE + width - latent_width)
    low, high = starts_ref[2 * ctx], starts_ref[2 * ctx + 1]

    if state_in:
        for to_ref, from_ref in zip((acc, top, total), state_in):
            to_ref[...] = from_ref[...]
    else:
        top[...] = jnp.full(top.shape, -1e30, jnp.float32)
        total[...] = jnp.zeros(total.shape, jnp.float32)
        acc[...] = jnp.zeros(acc.shape, jnp.float32)

    pieces = []
    for index, ref in enumerate(piece_refs):
        last, owner = lasts[index // 2], core if index % 2 == 0 else 1 - core
        for middle in range(4):
            px = (x + jnp.where(owner == 0, OFFSETS[last], OFFSETS[middle])) & 3
            py = (y + jnp.where(owner == 0, OFFSETS[middle], OFFSETS[last])) & 3
            for first in range(8):
                pz = (z + WINDOW[first]) & 7
                start = starts_ref[((px & 1) << 5) + (pz << 2) + (owner << 1) + (px >> 1)]
                pieces.append((ref, middle * 8 + first, start, py * PIECE))
    below = jnp.int32(0)
    within = jnp.int32(0)
    for _, _, start, _ in pieces:
        below = below + jnp.where(start <= low, 1, 0)
        within = within + jnp.where(start <= high, 1, 0)
    lane = lax.broadcasted_iota(jnp.int32, (PIECE, 64), 1)
    row = lax.broadcasted_iota(jnp.int32, (PIECE, 64), 0)
    unit, offset = jnp.where(lane == 0, 1, 0), jnp.where(lane == 1, row, 0)
    beside = jnp.where(lane == 1, 1, 0)
    nexts = [jnp.int32(0), below, within]
    for ref, at, start, shift in pieces:
        first, second = start <= low, start <= high
        to = jnp.where(first, nexts[0], jnp.where(second, nexts[1], nexts[2]))
        nexts[0] = nexts[0] + jnp.where(first, 1, 0)
        nexts[1] = nexts[1] + jnp.where(second & (start > low), 1, 0)
        nexts[2] = nexts[2] + jnp.where(second, 0, 1)
        to = pl.ds(pl.multiple_of(to * PIECE, PIECE), PIECE)
        keys[to, :width] = ref[at]
        mark = unit * (start >> 6) + offset + beside * shift
        keys[to, width:] = mark.astype(jnp.float32).astype(jnp.bfloat16)

    query_row = lax.broadcasted_iota(jnp.int32, (block, TILE), 0).astype(jnp.float32)
    per_tile = TILE // PIECE
    tiles_low = (below + per_tile - 1) >> 4
    tiles = tiles_low + ((within + per_tile - 1) >> 4)

    def place(index):
        is_high = index >= tiles_low
        half = jnp.where(is_high, 1, 0)
        at = jnp.minimum((index - half * tiles_low) * TILE, keys.shape[0] - TILE)
        start = jnp.where(is_high, high, low)
        return half, pl.multiple_of(at, TILE), start

    def score(buffer, index):
        half, at, start = place(index)
        s = lax.dot_general(
            query_ref[half],
            keys[pl.ds(at, TILE), :],
            (((1,), (1,)), ((), ())),
            preferred_element_type=jnp.float32,
        )
        position = jnp.broadcast_to(s[:1, :], (block, TILE))
        allowed = position - start.astype(jnp.float32) <= query_row
        s = s[PIECE:, :]
        s = jnp.where(allowed[None], s.reshape(rows // block, block, TILE), -1e30)
        buffer[...] = s.reshape(rows, TILE)

    def absorb_tile(buffer, index):
        half, at, _ = place(index)
        own = pl.ds(pl.multiple_of(half * rows, rows), rows)
        left, right = buffer[:, :128], buffer[:, 128:]
        old = top[own, :]
        new = jnp.maximum(old, jnp.max(jnp.maximum(left, right), axis=1, keepdims=True))
        scale = jnp.exp2((old - new) * factor)
        left = jnp.exp2((left - new) * factor)
        right = jnp.exp2((right - new) * factor)
        top[own, :] = new
        total[own, :] = total[own, :] * scale + (left + right)
        weights = jnp.concatenate([left, right], axis=1).astype(jnp.bfloat16)
        scales = jnp.concatenate([scale] * (latent_width // 128), axis=1)
        acc[own, :] = acc[own, :] * scales + jnp.dot(
            weights, keys[pl.ds(at, TILE), :latent_width], preferred_element_type=jnp.float32
        )

    score(even, 0)

    @pl.loop(0, tiles - 1)
    def _(index):
        @pl.when((index & 1) == 0)
        def _():
            score(odd, index + 1)
            absorb_tile(even, index)

        @pl.when((index & 1) == 1)
        def _():
            score(even, index + 1)
            absorb_tile(odd, index)

    @pl.when((tiles & 1) == 1)
    def _():
        absorb_tile(even, tiles - 1)

    @pl.when((tiles & 1) == 0)
    def _():
        absorb_tile(odd, tiles - 1)

    if finish:
        value_width = uv_ref.shape[2]
        for h in range(uv_ref.shape[0]):
            lat = []
            for half in range(2):
                own = slice(half * rows + h * block, half * rows + (h + 1) * block)
                whole = jnp.sum(total[own, :], axis=1, keepdims=True)
                lat.append((acc[own, :] / whole).astype(jnp.bfloat16))
            out_ref[:, h * value_width : (h + 1) * value_width] = jnp.dot(
                jnp.concatenate(lat), uv_ref[h], preferred_element_type=jnp.float32
            ).astype(jnp.bfloat16)


def absorb(lasts, finish, block_start, query, pieces, state, w_uv):
    heads, latent_width, value_width = w_uv.shape
    rows, width = query.shape[1] - PIECE, query.shape[2]
    count = sum(p.shape[0] * p.shape[1] for p in pieces)
    vmem = pl.BlockSpec(memory_space=pltpu.VMEM)
    state_shapes = [(2 * rows, latent_width), (2 * rows, 128), (2 * rows, 128)]
    scratch = [
        pltpu.VMEM((count, width), jnp.bfloat16),
        pltpu.VMEM((rows, TILE), jnp.float32),
        pltpu.VMEM((rows, TILE), jnp.float32),
    ]
    operands = [block_start, query, *pieces, *state]
    if finish:
        operands.append(w_uv)
        scratch += [pltpu.VMEM(shape, jnp.float32) for shape in state_shapes]
        out_shape = jax.ShapeDtypeStruct((2 * rows // heads, heads * value_width), jnp.bfloat16)
    else:
        out_shape = [jax.ShapeDtypeStruct(shape, jnp.float32) for shape in state_shapes]
    return pl.pallas_call(
        functools.partial(absorb_kernel, lasts, finish),
        in_specs=[pl.BlockSpec(memory_space=pltpu.SMEM)] + [vmem] * (len(operands) - 1),
        out_specs=vmem if finish else [vmem] * 3,
        out_shape=out_shape,
        scratch_shapes=scratch,
        compiler_params=pltpu.CompilerParams(vmem_limit_bytes=24 * 2**20),
        cost_estimate=pl.CostEstimate(
            flops=2 * rows * count * (width + latent_width),
            bytes_accessed=10 * 2**20,
            transcendentals=rows * count,
        ),
        name=f"absorb_{lasts[0]}",
    )(*operands)


def shards(q_nope, q_rope, latent, block_start, w_uk, w_uv):
    query = make_queries(q_nope, q_rope, w_uk)
    own, query = gather_own_core(latent, query)
    state = ()
    for lasts in GROUPS:
        chunks = [own[last] for last in lasts]
        if state:
            *chunks, state = lax.optimization_barrier((*chunks, state))
        pieces = [piece for chunk in chunks for piece in (chunk, other_core(chunk))]
        finish = lasts[-1] == len(own) - 1
        state = absorb(lasts, finish, block_start, query, pieces, state, w_uv)
    return state


def solution(mesh):
    placed = (P("ctx", "head"), P("ctx", "head"), P(BOTH, None), P(), P("head"), P("head"))
    return jax.shard_map(
        shards, mesh=mesh, in_specs=placed, out_specs=P("ctx", "head"), check_vma=False
    )
```

```python
import functools
import math

import jax
import jax.numpy as jnp
from jax import lax
from jax.experimental import pallas as pl
from jax.experimental.pallas import tpu as pltpu
from jax.sharding import PartitionSpec as P

BOTH = ("ctx", "head")
PIECE = 16
TILE = 256
NOPE = 128
GROUPS = ((0,), (1, 2), (3,))
OFFSETS = (0, 1, 3, 2)
WINDOW = (0, 1, 7, 3, 4, 2, 5, 6)


def device_index(x, y, z, core):
    return (((x % 2) * 8 + z) * 2 + core) * 8 + (x // 2) * 4 + y


def from_offset(value, first, second):
    pairs = []
    for x in range(4):
        for y in range(4):
            for z in range(8):
                for core in range(2):
                    dx, dy, dz = second if core else first
                    source = device_index((x + dx) % 4, (y + dy) % 4, (z + dz) % 8, core)
                    pairs.append((source, device_index(x, y, z, core)))
    return lax.ppermute(value, BOTH, pairs)


def other_core(value):
    return lax.ppermute(value, "ctx", [(i, i ^ 1) for i in range(32)])


def gather_own_core(latent, query):
    latent = latent[None]
    up = from_offset(latent, (0, 0, 1), (0, 0, 1))
    down = from_offset(latent, (0, 0, 7), (0, 0, 7))
    window = jnp.concatenate([latent, up, down])
    far_up = from_offset(window, (0, 0, 3), (0, 0, 3))
    far_down = from_offset(window, (0, 0, 5), (0, 0, 5))[:2]
    column = jnp.concatenate([window, far_up, far_down])
    lines = [from_offset(column, (0, d, 0), (d, 0, 0)) for d in OFFSETS[1:]]
    *lines, query = lax.optimization_barrier((*lines, query))
    plane = jnp.concatenate([column, *lines])
    lines = [from_offset(plane, (d, 0, 0), (0, d, 0)) for d in OFFSETS[1:]]
    return [plane, *lines], query


def query_kernel(nope_ref, rope_ref, uk_ref, query_ref):
    latent_width = uk_ref.shape[2]
    nope_width = uk_ref.shape[1]
    rope_width = rope_ref.shape[1] // uk_ref.shape[0]
    block = nope_ref.shape[0] // 2
    for head in range(uk_ref.shape[0]):
        lat = jnp.dot(
            nope_ref[:, head * nope_width : (head + 1) * nope_width],
            uk_ref[head],
            preferred_element_type=jnp.float32,
        ).astype(jnp.bfloat16)
        rope = rope_ref[:, head * rope_width : (head + 1) * rope_width]
        for half in range(2):
            rows = slice(half * block, (half + 1) * block)
            to = slice(head * block, (head + 1) * block)
            query_ref[half, to, :latent_width] = lat[rows]
            query_ref[half, to, latent_width:] = rope[rows]


def make_queries(q_nope, q_rope, w_uk):
    rows = q_nope.shape[0]
    heads, nope_width, latent_width = w_uk.shape
    rope_width = q_rope.shape[1] // heads
    width = latent_width + rope_width
    vmem = pl.BlockSpec(memory_space=pltpu.VMEM)
    return pl.pallas_call(
        query_kernel,
        in_specs=[vmem] * 3,
        out_specs=vmem,
        out_shape=jax.ShapeDtypeStruct((2, heads * rows // 2, width), jnp.bfloat16),
        compiler_params=pltpu.CompilerParams(vmem_limit_bytes=12 * 2**20),
        cost_estimate=pl.CostEstimate(
            flops=2 * rows * heads * nope_width * latent_width,
            bytes_accessed=6 * 2**20,
            transcendentals=0,
        ),
        name="make_queries",
    )(q_nope, q_rope, w_uk)


def absorb_kernel(lasts, finish, starts_ref, query_ref, *refs):
    piece_refs, refs = refs[: 2 * len(lasts)], refs[2 * len(lasts) :]
    state_in = refs[: 0 if lasts[0] == 0 else 3]
    refs = refs[len(state_in) :]
    if finish:
        uv_ref, out_ref, keys, marks, even, odd, acc, top, total = refs
    else:
        acc, top, total, keys, marks, even, odd = refs
    ctx, head_group = lax.axis_index("ctx"), lax.axis_index("head")
    x = (head_group >> 2) * 2 + (ctx >> 4)
    y, z, core = head_group & 3, (ctx >> 1) & 7, ctx & 1
    rows = query_ref.shape[1]
    block, width = 4 * PIECE, query_ref.shape[2]
    latent_width = acc.shape[1]
    factor = math.log2(math.e) / math.sqrt(NOPE + width - latent_width)
    low, high = starts_ref[2 * ctx], starts_ref[2 * ctx + 1]

    if state_in:
        for to_ref, from_ref in zip((acc, top, total), state_in):
            to_ref[...] = from_ref[...]
    else:
        top[...] = jnp.full(top.shape, -1e30, jnp.float32)
        total[...] = jnp.zeros(total.shape, jnp.float32)
        acc[...] = jnp.zeros(acc.shape, jnp.float32)

    pieces = []
    for index, ref in enumerate(piece_refs):
        last, owner = lasts[index // 2], core if index % 2 == 0 else 1 - core
        for middle in range(4):
            px = (x + jnp.where(owner == 0, OFFSETS[last], OFFSETS[middle])) & 3
            py = (y + jnp.where(owner == 0, OFFSETS[middle], OFFSETS[last])) & 3
            for first in range(8):
                pz = (z + WINDOW[first]) & 7
                start = starts_ref[((px & 1) << 5) + (pz << 2) + (owner << 1) + (px >> 1)]
                pieces.append((ref, middle * 8 + first, start, py * PIECE))
    below = jnp.int32(0)
    within = jnp.int32(0)
    for _, _, start, _ in pieces:
        below = below + jnp.where(start <= low, 1, 0)
        within = within + jnp.where(start <= high, 1, 0)
    lane = lax.broadcasted_iota(jnp.int32, (PIECE, 128), 1)
    row = lax.broadcasted_iota(jnp.int32, (PIECE, 128), 0)
    unit, offset = jnp.where(lane == 0, 1, 0), jnp.where(lane == 1, row, 0)
    beside = jnp.where(lane == 1, 1, 0)
    nexts = [jnp.int32(0), below, within]
    for ref, at, start, shift in pieces:
        first, second = start <= low, start <= high
        to = jnp.where(first, nexts[0], jnp.where(second, nexts[1], nexts[2]))
        nexts[0] = nexts[0] + jnp.where(first, 1, 0)
        nexts[1] = nexts[1] + jnp.where(second & (start > low), 1, 0)
        nexts[2] = nexts[2] + jnp.where(second, 0, 1)
        to = pl.ds(pl.multiple_of(to * PIECE, PIECE), PIECE)
        keys[to, :] = ref[at]
        mark = unit * (start >> 6) + offset + beside * shift
        marks[to, :] = mark.astype(jnp.float32).astype(jnp.bfloat16)

    read = jnp.where(lane == 0, float(block), jnp.where(lane == 1, 1.0, 0.0)).astype(jnp.bfloat16)
    query_row = lax.broadcasted_iota(jnp.int32, (block, TILE), 0).astype(jnp.float32)
    per_tile = TILE // PIECE
    tiles_low = (below + per_tile - 1) >> 4
    tiles = tiles_low + ((within + per_tile - 1) >> 4)

    def place(index):
        is_high = index >= tiles_low
        half = jnp.where(is_high, 1, 0)
        at = jnp.minimum((index - half * tiles_low) * TILE, keys.shape[0] - TILE)
        start = jnp.where(is_high, high, low)
        return half, pl.multiple_of(at, TILE), start

    def score(buffer, index):
        half, at, start = place(index)
        position = lax.dot_general(
            read,
            marks[pl.ds(at, TILE), :],
            (((1,), (1,)), ((), ())),
            preferred_element_type=jnp.float32,
        )
        position = jnp.broadcast_to(position[:1, :], (block, TILE))
        allowed = position - start.astype(jnp.float32) <= query_row
        s = lax.dot_general(
            query_ref[half],
            keys[pl.ds(at, TILE), :],
            (((1,), (1,)), ((), ())),
            preferred_element_type=jnp.float32,
        )
        s = jnp.where(allowed[None], s.reshape(rows // block, block, TILE), -1e30)
        buffer[...] = s.reshape(rows, TILE)

    def absorb_tile(buffer, index):
        half, at, _ = place(index)
        own = pl.ds(pl.multiple_of(half * rows, rows), rows)
        left, right = buffer[:, :128], buffer[:, 128:]
        old = top[own, :]
        new = jnp.maximum(old, jnp.max(jnp.maximum(left, right), axis=1, keepdims=True))
        scale = jnp.exp2((old - new) * factor)
        left = jnp.exp2((left - new) * factor)
        right = jnp.exp2((right - new) * factor)
        top[own, :] = new
        total[own, :] = total[own, :] * scale + (left + right)
        weights = jnp.concatenate([left, right], axis=1).astype(jnp.bfloat16)
        scales = jnp.concatenate([scale] * (latent_width // 128), axis=1)
        acc[own, :] = acc[own, :] * scales + jnp.dot(
            weights, keys[pl.ds(at, TILE), :latent_width], preferred_element_type=jnp.float32
        )

    score(even, 0)

    @pl.loop(0, tiles - 1)
    def _(index):
        @pl.when((index & 1) == 0)
        def _():
            score(odd, index + 1)
            absorb_tile(even, index)

        @pl.when((index & 1) == 1)
        def _():
            score(even, index + 1)
            absorb_tile(odd, index)

    @pl.when((tiles & 1) == 1)
    def _():
        absorb_tile(even, tiles - 1)

    @pl.when((tiles & 1) == 0)
    def _():
        absorb_tile(odd, tiles - 1)

    if finish:
        value_width = uv_ref.shape[2]
        for h in range(uv_ref.shape[0]):
            lat = []
            for half in range(2):
                own = slice(half * rows + h * block, half * rows + (h + 1) * block)
                share = 1.0 / jnp.sum(total[own, :], axis=1, keepdims=True)
                lat.append((acc[own, :] * share).astype(jnp.bfloat16))
            out_ref[:, h * value_width : (h + 1) * value_width] = jnp.dot(
                jnp.concatenate(lat), uv_ref[h], preferred_element_type=jnp.float32
            ).astype(jnp.bfloat16)


def absorb(lasts, finish, block_start, query, pieces, state, w_uv):
    heads, latent_width, value_width = w_uv.shape
    rows, width = query.shape[1:]
    count = sum(p.shape[0] * p.shape[1] for p in pieces)
    vmem = pl.BlockSpec(memory_space=pltpu.VMEM)
    state_shapes = [(2 * rows, latent_width), (2 * rows, 128), (2 * rows, 128)]
    scratch = [
        pltpu.VMEM((count, width), jnp.bfloat16),
        pltpu.VMEM((count, 128), jnp.bfloat16),
        pltpu.VMEM((rows, TILE), jnp.float32),
        pltpu.VMEM((rows, TILE), jnp.float32),
    ]
    operands = [block_start, query, *pieces, *state]
    if finish:
        operands.append(w_uv)
        scratch += [pltpu.VMEM(shape, jnp.float32) for shape in state_shapes]
        out_shape = jax.ShapeDtypeStruct((2 * rows // heads, heads * value_width), jnp.bfloat16)
    else:
        out_shape = [jax.ShapeDtypeStruct(shape, jnp.float32) for shape in state_shapes]
    return pl.pallas_call(
        functools.partial(absorb_kernel, lasts, finish),
        in_specs=[pl.BlockSpec(memory_space=pltpu.SMEM)] + [vmem] * (len(operands) - 1),
        out_specs=vmem if finish else [vmem] * 3,
        out_shape=out_shape,
        scratch_shapes=scratch,
        compiler_params=pltpu.CompilerParams(vmem_limit_bytes=24 * 2**20),
        cost_estimate=pl.CostEstimate(
            flops=2 * rows * count * (width + latent_width),
            bytes_accessed=10 * 2**20,
            transcendentals=rows * count,
        ),
        name=f"absorb_{lasts[0]}",
    )(*operands)


def shards(q_nope, q_rope, latent, block_start, w_uk, w_uv):
    query = make_queries(q_nope, q_rope, w_uk)
    own, query = gather_own_core(latent, query)
    state = ()
    for lasts in GROUPS:
        chunks = [own[last] for last in lasts]
        if state:
            *chunks, state = lax.optimization_barrier((*chunks, state))
        pieces = [piece for chunk in chunks for piece in (chunk, other_core(chunk))]
        finish = lasts[-1] == len(own) - 1
        state = absorb(lasts, finish, block_start, query, pieces, state, w_uv)
    return state


def solution(mesh):
    placed = (P("ctx", "head"), P("ctx", "head"), P(BOTH, None), P(), P("head"), P("head"))
    return jax.shard_map(
        shards, mesh=mesh, in_specs=placed, out_specs=P("ctx", "head"), check_vma=False
    )
```
